128 devices in a mesh: seq: 8 (over y, z_hi), res: 16 (over z_lo, x, core).
Axes of the slice: x: 4, y: 4, z: 4 (z_hi: 2, z_lo: 2; z = z_hi * 2 + z_lo), core: 2. Of those that a mesh axis runs over, the one named last changes fastest.
Arguments:
- tokens: bfloat16 [96, 1024, 768], P('seq', 'res'), may hold values from -8 to 8
- w_query: bfloat16 [768, 768], replicated, may hold values from -0.625 to 0.625
- w_keyval: bfloat16 [768, 1536], replicated, may hold values from -0.21875 to 0.21875
- w_out: bfloat16 [768, 768], replicated, may hold values from -0.21875 to 0.21875
Outputs:
- mixed: float32 [96, 1024, 768], P('seq', 'res')
The draws below stay inside these ranges and needn't reach their ends.
All inputs are finite; a program needn't handle non-finite values.
Results may differ from the reference program's by a relative error of at most 0.012.
Values may be sent and summed in bfloat16 or wider, within the bound.
A program may use at most 192 MiB of HBM per device.

```python
import math
import jax
import jax.numpy as jnp
from jax import lax

D = 768
HEADS = 12
DH = 64
RES_DEV = 64
SEQS = 96
RES = 1024


def draw_tokens(key, part):
    key = jax.random.fold_in(key, 11)
    key_base = jax.random.fold_in(key, 0)
    base = jax.random.normal(key_base, (SEQS, RES, D), jnp.float32)
    values = base
    return jnp.clip(values, -8.0, 8.0).astype(jnp.bfloat16)


def scatter_about(own_key, extent, spread, reach, held_as=jnp.bfloat16):
    return jnp.clip(spread * jax.random.normal(own_key, extent, jnp.float32), -reach, reach).astype(held_as)


def setup_inputs(seed: int = 0) -> dict:
    streams_of = jax.random.split(jax.random.key(seed), 5)
    tokens = draw_tokens(jax.random.fold_in(streams_of[4], 71), 0)
    w_query = scatter_about(streams_of[1], (D, D), (D // 9) ** -0.5, 0.625)
    w_keyval = scatter_about(streams_of[2], (D, 2 * D), D ** -0.5, 0.21875)
    w_out = scatter_about(streams_of[3], (D, D), D ** -0.5, 0.21875)
    return dict(tokens=tokens, w_query=w_query, w_keyval=w_keyval, w_out=w_out)


def reference(tokens, w_query, w_keyval, w_out):
    flat = tokens.reshape(SEQS * RES, D)
    scale = 1.0 / math.sqrt(DH * SEQS)
    query = (jnp.dot(flat, w_query, preferred_element_type=jnp.float32) * scale).astype(jnp.bfloat16)
    keyval = jnp.dot(flat, w_keyval, preferred_element_type=jnp.float32).astype(jnp.bfloat16)
    keys = keyval[:, :D].reshape(SEQS, RES, HEADS, DH).astype(jnp.float32)
    values = keyval[:, D:].reshape(SEQS, RES, HEADS, DH).astype(jnp.float32)
    query = query.reshape(SEQS, RES // RES_DEV, RES_DEV, HEADS, DH).transpose(1, 0, 2, 3, 4)

    def one_block(query_block):
        logits = jnp.einsum('sihd,sjhd->hij', query_block.astype(jnp.float32), keys)
        largest = lax.optimization_barrier(jnp.max(logits, axis=-1, keepdims=True))
        weights = jnp.exp(logits - largest)
        probs = (weights / lax.optimization_barrier(jnp.sum(weights, axis=-1, keepdims=True))).astype(jnp.bfloat16)
        attended = jnp.einsum('hij,sjhd->sihd', probs.astype(jnp.float32), values)
        return attended.astype(jnp.bfloat16)
    attended = lax.map(one_block, query)
    attended = attended.transpose(1, 0, 2, 3, 4).reshape(SEQS * RES, D)
    mixed = jnp.dot(attended, w_out, preferred_element_type=jnp.float32)
    return mixed.reshape(SEQS, RES, D)
```

```python
import functools
import math

import jax
import jax.numpy as jnp
from jax import lax
from jax.experimental import pallas as pl
from jax.experimental.pallas import tpu as pltpu
from jax.sharding import PartitionSpec as P

DH = 64
NX, NY = 4, 4
MESH = pl.DeviceIdType.MESH
BF16, F32 = jnp.bfloat16, jnp.float32


def layer_kernel(
    scale,
    tok_hbm, wq_hbm, wkv_hbm, out_ref,
    tok, wq, wkv, q_mine, k_mine, v_mine, q_all, k_all, v_all,
    scores, part_out, part_in, own_rows, pair_out, pair_in, probs, att_out, att_all,
    load_sem, send_sem, recv_sem,
):
    seq, res = lax.axis_index("seq"), lax.axis_index("res")
    y, zh = lax.div(seq, 2), lax.rem(seq, 2)
    zl, x, c = lax.div(res, 8), lax.rem(lax.div(res, 2), NX), lax.rem(res, 2)
    width = tok.shape[1]
    heads = q_mine.shape[0]
    per = heads // NX
    cols = 256

    def at_x(k):
        return (seq, zl * 8 + lax.rem(x + k, NX) * 2 + c)

    def at_y(k):
        return (lax.rem(y + k, NY) * 2 + zh, res)

    at_zl = (seq, (1 - zl) * 8 + x * 2 + c)
    at_core = (seq, zl * 8 + x * 2 + (1 - c))
    at_zh = (y * 2 + (1 - zh), res)

    copies = {}

    def send(kind, slot, hh, k, src, dst, where):
        copy = pltpu.make_async_remote_copy(
            src_ref=src, dst_ref=dst,
            send_sem=send_sem.at[slot, hh, k], recv_sem=recv_sem.at[slot, hh, k],
            device_id=where, device_id_type=MESH,
        )
        copy.start()
        copies[kind, hh, k] = copy

    def arrived(kind, hh, k):
        copies[kind, hh, k].wait_recv()

    half = wkv.shape[1] // 2
    loads = [
        pltpu.make_async_copy(tok_hbm, tok, load_sem.at[0]),
        pltpu.make_async_copy(wkv_hbm.at[:, pl.ds(0, half)], wkv.at[:, pl.ds(0, half)], load_sem.at[1]),
        pltpu.make_async_copy(wq_hbm, wq, load_sem.at[2]),
        pltpu.make_async_copy(wkv_hbm.at[:, pl.ds(half, half)], wkv.at[:, pl.ds(half, half)], load_sem.at[3]),
    ]
    for load in loads:
        load.start()

    barrier = pltpu.get_barrier_semaphore()
    others = [at_x(1), at_x(2), at_x(3), at_y(1), at_y(2), at_y(3), at_zl, at_core, at_zh]
    for other in others:
        pl.semaphore_signal(barrier, inc=1, device_id=other, device_id_type=MESH)

    def low_lanes(rows):
        return lax.broadcasted_iota(jnp.int32, (rows, 128), 1) < DH

    def project(w, first, dst, factor):
        low = low_lanes(64)

        @pl.loop(0, width // cols)
        def _(n):
            at = pl.multiple_of(first + n * cols, cols)
            acc = jnp.dot(tok[...], w[:, pl.ds(at, cols)], preferred_element_type=F32)
            if factor is not None:
                acc = acc * factor
            for pair in range(cols // 128):
                for m in range(tok.shape[0] // 128):
                    even = acc[m * 128:m * 128 + 64, pair * 128:pair * 128 + 128]
                    odd = pltpu.roll(acc[m * 128 + 64:m * 128 + 128, pair * 128:pair * 128 + 128], 64, 1)
                    head = n * (cols // DH) + 2 * pair
                    dst[head, :, m * 128:m * 128 + 128] = jnp.where(low, even, odd).astype(BF16)
                    dst[head + 1, :, m * 128:m * 128 + 128] = jnp.where(low, odd, even).astype(BF16)

    mine = c * 2 + zl
    theirs = c * 2 + (1 - zl)

    def kv_send(kind, slot, src, dst, hh):
        dst[hh, mine, x] = src[per * x + hh]
        for k in (1, 3, 2):
            to = lax.rem(x + k, NX)
            send(kind + "x", slot, hh, k, src.at[per * to + hh], dst.at[hh, mine, x], at_x(k))

    def kv_own(kind, slot, src, dst, hh):
        send(kind + "z", slot + 1, hh, 0, src.at[per * x + hh], dst.at[hh, mine, x], at_zl)

    def kv_forward(kind, slot, dst, hh):
        for k in (1, 3, 2):
            arrived(kind + "x", hh, k)
            block = dst.at[hh, mine, lax.rem(x + NX - k, NX)]
            send(kind + "z", slot + 1, hh, k, block, block, at_zl)
        send(kind + "c", slot + 2, hh, 0, dst.at[hh, mine], dst.at[hh, mine], at_core)

    def kv_last(kind, slot, dst, hh):
        for k in (0, 1, 3, 2):
            arrived(kind + "z", hh, k)
        send(kind + "c", slot + 2, hh, 1, dst.at[hh, theirs], dst.at[hh, theirs], at_core)
        arrived(kind + "c", hh, 0)
        arrived(kind + "c", hh, 1)

    def q_send(hh):
        q_all[hh, x] = q_mine[per * x + hh]
        for k in (2, 1, 3):
            to = lax.rem(x + k, NX)
            send("q", 6, hh, k, q_mine.at[per * to + hh], q_all.at[hh, x], at_x(k))

    def logits(hh):
        for k in (2, 1, 3):
            arrived("q", hh, k)

        @pl.loop(0, 4)
        def _(t):
            s = lax.dot_general(
                q_all[hh].reshape(256, width), k_all[hh, t].reshape(256, width),
                (((1,), (1,)), ((), ())), preferred_element_type=F32,
            ).reshape(NX, 64, 256)
            at = pl.ds(pl.multiple_of(t * 256, 256), 256)
            scores[:, :, at] = s
            part_out[hh, :, :, at] = s.astype(BF16)

        own_rows[hh] = scores[y]
        for k in (2, 1, 3):
            send("r", 7, hh, k, part_out.at[hh, lax.rem(y + k, NY)], part_in.at[hh, k - 1], at_y(k))

    def add_rows(hh):
        for k in (2, 1, 3):
            arrived("r", hh, k)
        total = own_rows[hh]
        for k in range(3):
            total = total + part_in[hh, k].astype(F32)
        own_rows[hh] = total
        pair_out[hh] = total.astype(BF16)
        send("p", 8, hh, 0, pair_out.at[hh], pair_in.at[hh], at_zh)

    def softmax(hh):
        arrived("p", hh, 0)
        rows = own_rows[hh] + pair_in[hh].astype(F32)
        weights = jnp.exp(rows - jnp.max(rows, axis=-1, keepdims=True))
        probs[hh, y] = (weights / jnp.sum(weights, axis=-1, keepdims=True)).astype(BF16)
        for k in (2, 1, 3):
            send("a", 9, hh, k, probs.at[hh, y], probs.at[hh, y], at_y(k))

    def attend(hh):
        for k in (2, 1, 3):
            arrived("a", hh, k)

        @pl.loop(0, width // cols)
        def _(n):
            at = pl.ds(pl.multiple_of(n * cols, cols), cols)
            o = jnp.dot(
                probs[hh].reshape(256, 1024), v_all[hh, :, :, :, at].reshape(1024, cols),
                preferred_element_type=F32,
            )
            att_out[hh, :, :, at] = o.astype(BF16).reshape(NX, 64, cols)

        att_all[per * x + hh] = att_out[hh, x]
        for k in (2, 1, 3):
            to = lax.rem(x + k, NX)
            send("o", 10, hh, k, att_out.at[hh, to], att_all.at[per * x + hh], at_x(k))

    loads[0].wait()
    loads[1].wait()
    project(wkv, 0, k_mine, None)
    pl.semaphore_wait(barrier, len(others))
    kv_send("k", 0, k_mine, k_all, 0)
    kv_own("k", 0, k_mine, k_all, 0)
    loads[2].wait()
    project(wq, 0, q_mine, scale)
    q_send(0)
    for hh in range(1, per):
        kv_send("k", 0, k_mine, k_all, hh)
        q_send(hh)
    loads[3].wait()
    project(wkv, half, v_mine, None)
    for hh in range(per):
        kv_send("v", 3, v_mine, v_all, hh)

    kv_forward("k", 0, k_all, 0)
    kv_own("k", 0, k_mine, k_all, 1)
    kv_last("k", 0, k_all, 0)
    logits(0)
    kv_forward("k", 0, k_all, 1)
    kv_own("k", 0, k_mine, k_all, 2)
    add_rows(0)
    kv_last("k", 0, k_all, 1)
    logits(1)
    kv_forward("k", 0, k_all, 2)
    softmax(0)
    kv_own("v", 3, v_mine, v_all, 0)
    add_rows(1)
    kv_last("k", 0, k_all, 2)
    logits(2)
    kv_forward("v", 3, v_all, 0)
    softmax(1)
    kv_own("v", 3, v_mine, v_all, 1)
    add_rows(2)
    kv_last("v", 3, v_all, 0)
    attend(0)
    kv_forward("v", 3, v_all, 1)
    softmax(2)
    kv_own("v", 3, v_mine, v_all, 2)
    kv_forward("v", 3, v_all, 2)
    kv_last("v", 3, v_all, 1)
    attend(1)
    kv_last("v", 3, v_all, 2)
    attend(2)

    for hh in range(per):
        for k in (2, 1, 3):
            arrived("o", hh, k)
    low = low_lanes(64)
    for pair in range(heads // 2):
        at = pl.ds(pair * 128, 128)
        for m in range(width // 128):
            a = att_all[2 * pair, :, m * 128:m * 128 + 128].astype(F32)
            b = att_all[2 * pair + 1, :, m * 128:m * 128 + 128].astype(F32)
            out_ref[m * 128:m * 128 + 64, at] = jnp.where(low, a, b).astype(BF16)
            out_ref[m * 128 + 64:m * 128 + 128, at] = pltpu.roll(jnp.where(low, b, a), 64, 1).astype(BF16)
    for copy in copies.values():
        copy.wait_send()


def local(tokens, w_query, w_keyval, w_out):
    seq_dev, res_dev, width = tokens.shape
    heads = width // DH
    per = heads // NX
    scale = 1.0 / math.sqrt(DH * seq_dev * lax.axis_size("seq"))
    flat = tokens.reshape(seq_dev * res_dev, width)
    rows = seq_dev * res_dev
    any_spec = pl.BlockSpec(memory_space=pl.ANY)
    block = (heads, res_dev, seq_dev * DH)
    attended = pl.pallas_call(
        functools.partial(layer_kernel, scale),
        out_shape=jax.ShapeDtypeStruct((rows, width), BF16),
        in_specs=[any_spec] * 3,
        out_specs=pl.BlockSpec(memory_space=pltpu.VMEM),
        scratch_shapes=[
            pltpu.VMEM((rows, width), BF16),
            pltpu.VMEM((width, width), BF16),
            pltpu.VMEM((width, 2 * width), BF16),
            pltpu.VMEM(block, BF16),
            pltpu.VMEM(block, BF16),
            pltpu.VMEM(block, BF16),
            pltpu.VMEM((per, NX, res_dev, seq_dev * DH), BF16),
            pltpu.VMEM((per, 4, NX, res_dev, seq_dev * DH), BF16),
            pltpu.VMEM((per, 4, NX, res_dev, seq_dev * DH), BF16),
            pltpu.VMEM((NX, res_dev, 1024), F32),
            pltpu.VMEM((per, NY, res_dev, 1024), BF16),
            pltpu.VMEM((per, 3, res_dev, 1024), BF16),
            pltpu.VMEM((per, res_dev, 1024), F32),
            pltpu.VMEM((per, res_dev, 1024), BF16),
            pltpu.VMEM((per, res_dev, 1024), BF16),
            pltpu.VMEM((per, NY, res_dev, 1024), BF16),
            pltpu.VMEM((per, NX, res_dev, seq_dev * DH), BF16),
            pltpu.VMEM(block, BF16),
            pltpu.SemaphoreType.DMA((4,)),
            pltpu.SemaphoreType.DMA((11, per, 4)),
            pltpu.SemaphoreType.DMA((11, per, 4)),
        ],
        cost_estimate=pl.CostEstimate(flops=5 * 10**9, bytes_accessed=10**7, transcendentals=2 * 10**5),
        compiler_params=pltpu.CompilerParams(
            collective_id=0, has_side_effects=True, vmem_limit_bytes=56 * 2**20
        ),
        name="tied_row_attention",
    )(flat, w_query, w_keyval)
    mixed = jnp.dot(attended, w_out, preferred_element_type=F32)
    return mixed.reshape(seq_dev, res_dev, width)


def solution(mesh):
    return jax.shard_map(
        local,
        mesh=mesh,
        in_specs=(P("seq", "res", None), P(), P(), P()),
        out_specs=P("seq", "res", None),
        check_vma=False,
    )
```

```python
import functools
import math

import jax
import jax.numpy as jnp
from jax import lax
from jax.experimental import pallas as pl
from jax.experimental.pallas import tpu as pltpu
from jax.sharding import PartitionSpec as P

DH = 64
NX, NY = 4, 4
COLS = 256
MORE = 128
MESH = pl.DeviceIdType.MESH
BF16, F32 = jnp.bfloat16, jnp.float32


def layer_kernel(
    scale,
    tok_hbm, wq_hbm, wkv_hbm, wout_hbm, out_hbm,
    tok, wq, wkv, wout, q_mine, k_mine, v_mine, k_more, v_more, q_all, k_all, v_all,
    scores, part_out, part_in, own_rows, pair_out, pair_in, probs, att_out, att_all, left, mixed,
    load_sem, send_sem, recv_sem,
):
    seq, res = lax.axis_index("seq"), lax.axis_index("res")
    y, zh = lax.div(seq, 2), lax.rem(seq, 2)
    zl, x, c = lax.div(res, 8), lax.rem(lax.div(res, 2), NX), lax.rem(res, 2)
    rows, width = tok_hbm.shape
    heads = q_mine.shape[0]
    per = heads // NX

    def at_x(k):
        return (seq, zl * 8 + lax.rem(x + k, NX) * 2 + c)

    def at_y(k):
        return (lax.rem(y + k, NY) * 2 + zh, res)

    at_zl = (seq, (1 - zl) * 8 + x * 2 + c)
    at_core = (seq, zl * 8 + x * 2 + (1 - c))
    at_zh = (y * 2 + (1 - zh), res)

    copies = {}
    seen = set()
    slots = ["kx", "kz", "kc", "kt", "vx", "vz", "vc", "vt", "q", "r", "p", "a", "o", "t"]

    def send(kind, stage, k, src, dst, where):
        slot = slots.index(kind)
        copy = pltpu.make_async_remote_copy(
            src_ref=src, dst_ref=dst,
            send_sem=send_sem.at[slot, stage, k], recv_sem=recv_sem.at[slot, stage, k],
            device_id=where, device_id_type=MESH,
        )
        copy.start()
        copies[kind, stage, k] = copy

    def arrived(kind, stage, *ks):
        for k in ks:
            if (kind, stage, k) not in seen:
                seen.add((kind, stage, k))
                copies[kind, stage, k].wait_recv()

    half = wkv.shape[1] // 2
    loads = [
        pltpu.make_async_copy(tok_hbm.at[pl.ds(0, 128)], tok.at[pl.ds(0, 128)], load_sem.at[0]),
        pltpu.make_async_copy(tok_hbm.at[pl.ds(128, rows - 128)], tok.at[pl.ds(128, rows - 128)], load_sem.at[1]),
        pltpu.make_async_copy(wkv_hbm.at[:, pl.ds(0, half)], wkv.at[:, pl.ds(0, half)], load_sem.at[2]),
        pltpu.make_async_copy(wq_hbm, wq, load_sem.at[3]),
        pltpu.make_async_copy(wkv_hbm.at[:, pl.ds(half, half)], wkv.at[:, pl.ds(half, half)], load_sem.at[4]),
    ] + [pltpu.make_async_copy(wout_hbm.at[:, hh], wout.at[hh], load_sem.at[5 + hh]) for hh in range(per)]
    for load in loads[:3]:
        load.start()

    barrier = pltpu.get_barrier_semaphore()
    others = [at_x(1), at_x(2), at_x(3), at_y(1), at_y(2), at_y(3), at_zl, at_core, at_zh]
    for other in others:
        pl.semaphore_signal(barrier, inc=1, device_id=other, device_id_type=MESH)
    for load in loads[3:]:
        load.start()

    low = lax.broadcasted_iota(jnp.int32, (64, 128), 1) < DH

    def project(w, first, dst, factor=None, row=0, pairs=rows // 128):
        @pl.loop(0, width // COLS)
        def _(n):
            at = pl.multiple_of(first + n * COLS, COLS)
            acc = jnp.dot(tok[row:row + pairs * 128], w[:, pl.ds(at, COLS)], preferred_element_type=F32)
            if factor is not None:
                acc = acc * factor
            for pair in range(COLS // 128):
                for m in range(pairs):
                    even = acc[m * 128:m * 128 + 64, pair * 128:pair * 128 + 128]
                    odd = pltpu.roll(acc[m * 128 + 64:m * 128 + 128, pair * 128:pair * 128 + 128], 64, 1)
                    head = n * (COLS // DH) + 2 * pair
                    dst[head, :, m * 128:m * 128 + 128] = jnp.where(low, even, odd).astype(BF16)
                    dst[head + 1, :, m * 128:m * 128 + 128] = jnp.where(low, odd, even).astype(BF16)

    mine = c * 2 + zl
    theirs = c * 2 + (1 - zl)
    kv = {"k": (k_mine, k_all, k_more), "v": (v_mine, v_all, v_more)}

    def columns(stage):
        return {2: (2, 0, width), 3: (2, 0, 512), 4: (2, 512, 256)}.get(stage, (stage, 0, width))

    def kv_send(kind, hh):
        src, dst, _ = kv[kind]
        dst[hh, mine, x] = src[per * x + hh]
        for k in (1, 3, 2):
            to = lax.rem(x + k, NX)
            send(kind + "x", hh, k, src.at[per * to + hh], dst.at[hh, mine, x], at_x(k))

    def kv_more(kind):
        arrived("t", 0, 0)
        _, dst, src = kv[kind]
        project(wkv, 0 if kind == "k" else half, src, row=rows, pairs=1)
        for hh in range(per):
            dst[hh, theirs, x, :, 0:MORE] = src[per * x + hh]
        for k in (2, 1, 3):
            to = lax.rem(x + k, NX)
            send(
                kind + "t", 0, k, src.at[pl.ds(per * to, per)],
                dst.at[pl.ds(0, per), theirs, x, :, pl.ds(0, MORE)], at_x(k),
            )

    def across(stage):
        hh, lo, n = columns(stage)
        first = max(lo, MORE)
        return hh, pl.ds(first, lo + n - first)

    def kv_own(kind, stage):
        src, dst, _ = kv[kind]
        hh, at = across(stage)
        send(kind + "z", stage, 0, src.at[per * x + hh, :, at], dst.at[hh, mine, x, :, at], at_zl)

    def kv_forward(kind, stage):
        _, dst, _ = kv[kind]
        hh, at = across(stage)
        for k in (1, 3, 2):
            arrived(kind + "x", hh, k)
            block = dst.at[hh, mine, lax.rem(x + NX - k, NX), :, at]
            send(kind + "z", stage, k, block, block, at_zl)
        hh, lo, n = columns(stage)
        blocks = dst.at[hh, mine, :, :, pl.ds(lo, n)]
        send(kind + "c", stage, 0, blocks, blocks, at_core)

    def kv_last(kind, stage):
        _, dst, _ = kv[kind]
        arrived(kind + "t", 0, 2, 1, 3)
        arrived(kind + "z", stage, 0, 1, 3, 2)
        hh, lo, n = columns(stage)
        blocks = dst.at[hh, theirs, :, :, pl.ds(lo, n)]
        send(kind + "c", stage, 1, blocks, blocks, at_core)
        arrived(kind + "c", stage, 0, 1)

    def q_send(hh):
        q_all[hh, x] = q_mine[per * x + hh]
        for k in (2, 1, 3):
            to = lax.rem(x + k, NX)
            send("q", hh, k, q_mine.at[per * to + hh], q_all.at[hh, x], at_x(k))

    def logits(hh):
        arrived("q", hh, 2, 1, 3)

        @pl.loop(0, 4)
        def _(t):
            s = lax.dot_general(
                q_all[hh].reshape(256, width), k_all[hh, t].reshape(256, width),
                (((1,), (1,)), ((), ())), preferred_element_type=F32,
            ).reshape(NX, 64, 256)
            at = pl.ds(pl.multiple_of(t * 256, 256), 256)
            scores[:, :, at] = s
            part_out[hh, :, :, at] = s.astype(BF16)

        own_rows[hh] = scores[y]
        for k in (2, 1, 3):
            send("r", hh, k, part_out.at[hh, lax.rem(y + k, NY)], part_in.at[hh, k - 1], at_y(k))

    def add_rows(hh):
        arrived("r", hh, 2, 1, 3)
        total = own_rows[hh]
        for k in range(3):
            total = total + part_in[hh, k].astype(F32)
        own_rows[hh] = total
        pair_out[hh] = total.astype(BF16)
        send("p", hh, 0, pair_out.at[hh], pair_in.at[hh], at_zh)

    def softmax(hh):
        arrived("p", hh, 0)
        total = own_rows[hh] + pair_in[hh].astype(F32)
        weights = jnp.exp(total - jnp.max(total, axis=-1, keepdims=True))
        probs[hh, y] = (weights / jnp.sum(weights, axis=-1, keepdims=True)).astype(BF16)
        for k in (2, 1, 3):
            send("a", hh, k, probs.at[hh, y], probs.at[hh, y], at_y(k))

    def attend(stage):
        hh, lo, n = columns(stage)
        arrived("a", hh, 2, 1, 3)

        @pl.loop(lo // COLS, (lo + n) // COLS)
        def _(tile):
            at = pl.ds(pl.multiple_of(tile * COLS, COLS), COLS)
            o = jnp.dot(
                probs[hh].reshape(256, 1024), v_all[hh, :, :, :, at].reshape(1024, COLS),
                preferred_element_type=F32,
            )
            att_out[hh, :, :, at] = o.astype(BF16).reshape(NX, 64, COLS)

        at = pl.ds(lo, n)
        att_all[per * x + hh, :, at] = att_out[hh, x, :, at]
        for k in (2, 1, 3):
            to = lax.rem(x + k, NX)
            send("o", stage, k, att_out.at[hh, to, :, at], att_all.at[per * x + hh, :, at], at_x(k))

    def project_out(stage):
        hh, lo, n = columns(stage)
        arrived("o", stage, 2, 1, 3)
        if stage == 0:
            for load in loads[5:]:
                load.wait()
        for m in range(lo // 128, (lo + n) // 128):
            for pair in range(NX // 2):
                a = att_all[2 * pair * per + hh, :, m * 128:m * 128 + 128].astype(F32)
                b = att_all[(2 * pair + 1) * per + hh, :, m * 128:m * 128 + 128].astype(F32)
                halves = [jnp.where(low, a, b), pltpu.roll(jnp.where(low, b, a), 64, 1)]
                for s in range(2):
                    left[m * 128 + s * 64:m * 128 + s * 64 + 64, pair * 128:pair * 128 + 128] = halves[
                        (s + hh) % 2
                    ].astype(BF16)
        part = pl.ds(lo, n)

        @pl.loop(0, width // COLS)
        def _(tile):
            at = pl.ds(pl.multiple_of(tile * COLS, COLS), COLS)
            o = jnp.dot(left[part, :], wout[hh, :, :, at].reshape(NX * DH, COLS), preferred_element_type=F32)
            mixed[part, at] = o if hh == 0 else mixed[part, at] + o

    def store(stage):
        _, lo, n = columns(stage)
        copy = pltpu.make_async_copy(mixed.at[pl.ds(lo, n)], out_hbm.at[pl.ds(lo, n)], load_sem.at[5 + stage])
        copy.start()
        return copy

    def start_tokens():
        loads[0].wait()
        pl.semaphore_wait(barrier, len(others))
        send("t", 0, 0, tok.at[pl.ds(0, 128)], tok.at[pl.ds(rows, 128)], at_zl)

    def project_keys():
        loads[1].wait()
        loads[2].wait()
        project(wkv, 0, k_mine)

    def project_query():
        loads[3].wait()
        project(wq, 0, q_mine, scale)

    def project_values():
        loads[4].wait()
        project(wkv, half, v_mine)

    start_tokens()
    project_keys()
    kv_send("k", 0)
    kv_own("k", 0)
    kv_own("k", 1)
    project_query()
    kv_send("k", 1)
    kv_more("k")
    kv_forward("k", 0)
    q_send(0)
    kv_send("k", 2)
    q_send(1)
    kv_own("k", 2)
    project_values()
    q_send(2)
    kv_forward("k", 1)
    kv_send("v", 0)
    kv_send("v", 1)
    kv_own("v", 4)
    kv_last("k", 0)
    logits(0)
    kv_send("v", 2)
    kv_forward("k", 2)
    kv_more("v")
    kv_last("k", 1)
    kv_own("v", 0)
    logits(1)
    add_rows(0)
    kv_last("k", 2)
    kv_own("v", 1)
    logits(2)
    kv_forward("v", 0)
    softmax(0)
    add_rows(1)
    add_rows(2)
    kv_forward("v", 1)
    kv_forward("v", 3)
    softmax(1)
    kv_last("v", 0)
    kv_own("v", 3)
    softmax(2)
    kv_forward("v", 4)
    attend(0)
    kv_last("v", 1)
    attend(1)
    kv_last("v", 3)
    attend(3)
    kv_last("v", 4)
    attend(4)
    project_out(0)
    project_out(1)
    project_out(3)
    project_out(4)

    stores = [store(3), store(4)]
    for copy in copies.values():
        copy.wait_send()
    for copy in stores:
        copy.wait()


def local(tokens, w_query, w_keyval, w_out):
    seq_dev, res_dev, width = tokens.shape
    heads = width // DH
    per = heads // NX
    scale = 1.0 / math.sqrt(DH * seq_dev * lax.axis_size("seq"))
    rows = seq_dev * res_dev
    block = (heads, res_dev, seq_dev * DH)
    mixed = pl.pallas_call(
        functools.partial(layer_kernel, scale),
        out_shape=jax.ShapeDtypeStruct((rows, width), F32),
        in_specs=[pl.BlockSpec(memory_space=pltpu.HBM)] * 4,
        out_specs=pl.BlockSpec(memory_space=pl.ANY),
        scratch_shapes=[
            pltpu.VMEM((rows + 128, width), BF16),
            pltpu.VMEM((width, width), BF16),
            pltpu.VMEM((width, 2 * width), BF16),
            pltpu.VMEM((per, NX, DH, width), BF16),
            pltpu.VMEM(block, BF16),
            pltpu.VMEM(block, BF16),
            pltpu.VMEM(block, BF16),
            pltpu.VMEM((heads, res_dev, MORE), BF16),
            pltpu.VMEM((heads, res_dev, MORE), BF16),
            pltpu.VMEM((per, NX, res_dev, seq_dev * DH), BF16),
            pltpu.VMEM((per, 4, NX, res_dev, seq_dev * DH), BF16),
            pltpu.VMEM((per, 4, NX, res_dev, seq_dev * DH), BF16),
            pltpu.VMEM((NX, res_dev, 1024), F32),
            pltpu.VMEM((per, NY, res_dev, 1024), BF16),
            pltpu.VMEM((per, 3, res_dev, 1024), BF16),
            pltpu.VMEM((per, res_dev, 1024), F32),
            pltpu.VMEM((per, res_dev, 1024), BF16),
            pltpu.VMEM((per, res_dev, 1024), BF16),
            pltpu.VMEM((per, NY, res_dev, 1024), BF16),
            pltpu.VMEM((per, NX, res_dev, seq_dev * DH), BF16),
            pltpu.VMEM(block, BF16),
            pltpu.VMEM((rows, NX * DH), BF16),
            pltpu.VMEM((rows, width), F32),
            pltpu.SemaphoreType.DMA((10,)),
            pltpu.SemaphoreType.DMA((14, 5, 4)),
            pltpu.SemaphoreType.DMA((14, 5, 4)),
        ],
        cost_estimate=pl.CostEstimate(flops=6 * 10**9, bytes_accessed=10**7, transcendentals=2 * 10**5),
        compiler_params=pltpu.CompilerParams(
            collective_id=0, has_side_effects=True, vmem_limit_bytes=44 * 2**20
        ),
        name="tied_row_attention",
    )(tokens.reshape(rows, width), w_query, w_keyval, w_out.reshape(NX, per, DH, width))
    return mixed.reshape(seq_dev, res_dev, width)


def solution(mesh):
    return jax.shard_map(
        local,
        mesh=mesh,
        in_specs=(P("seq", "res", None), P(), P(), P()),
        out_specs=P("seq", "res", None),
        check_vma=False,
    )
```

```python
import functools
import math

import jax
import jax.numpy as jnp
from jax import lax
from jax.experimental import pallas as pl
from jax.experimental.pallas import tpu as pltpu
from jax.sharding import PartitionSpec as P

DH = 64
NX, NY = 4, 4
COLS = 256
MORE = 128
MESH = pl.DeviceIdType.MESH
BF16, F32 = jnp.bfloat16, jnp.float32


def layer_kernel(
    scale,
    tok_hbm, wq_hbm, wkv_hbm, wout_hbm, out_hbm,
    tok, wq, wkv, wout, q_mine, k_mine, v_mine, k_more, v_more, q_all, k_all, v_all,
    scores, part_out, part_in, own_rows, pair_out, pair_in, probs, att_out, att_all, left, mixed,
    load_sem, send_sem, recv_sem,
):
    seq, res = lax.axis_index("seq"), lax.axis_index("res")
    y, zh = lax.div(seq, 2), lax.rem(seq, 2)
    zl, x, c = lax.div(res, 8), lax.rem(lax.div(res, 2), NX), lax.rem(res, 2)
    rows, width = tok_hbm.shape
    heads = q_mine.shape[0]
    per = heads // NX

    def at_x(k):
        return (seq, zl * 8 + lax.rem(x + k, NX) * 2 + c)

    def at_y(k):
        return (lax.rem(y + k, NY) * 2 + zh, res)

    at_zl = (seq, (1 - zl) * 8 + x * 2 + c)
    at_core = (seq, zl * 8 + x * 2 + (1 - c))
    at_zh = (y * 2 + (1 - zh), res)

    copies = {}
    seen = set()
    slots = ["kx", "kz", "kc", "kt", "vx", "vz", "vc", "vt", "q", "r", "s", "p", "a", "b", "o", "t"]

    def send(kind, stage, k, src, dst, where):
        slot = slots.index(kind)
        copy = pltpu.make_async_remote_copy(
            src_ref=src, dst_ref=dst,
            send_sem=send_sem.at[slot, stage, k], recv_sem=recv_sem.at[slot, stage, k],
            device_id=where, device_id_type=MESH,
        )
        copy.start()
        copies[kind, stage, k] = copy

    def arrived(kind, stage, *ks):
        for k in ks:
            if (kind, stage, k) not in seen:
                seen.add((kind, stage, k))
                copies[kind, stage, k].wait_recv()

    half = wkv.shape[1] // 2
    loads = [
        pltpu.make_async_copy(tok_hbm.at[pl.ds(0, 128)], tok.at[pl.ds(0, 128)], load_sem.at[0]),
        pltpu.make_async_copy(tok_hbm.at[pl.ds(128, rows - 128)], tok.at[pl.ds(128, rows - 128)], load_sem.at[1]),
        pltpu.make_async_copy(wkv_hbm.at[:, pl.ds(0, half)], wkv.at[:, pl.ds(0, half)], load_sem.at[2]),
        pltpu.make_async_copy(wq_hbm, wq, load_sem.at[3]),
        pltpu.make_async_copy(wkv_hbm.at[:, pl.ds(half, half)], wkv.at[:, pl.ds(half, half)], load_sem.at[4]),
    ] + [pltpu.make_async_copy(wout_hbm.at[:, hh], wout.at[0, hh], load_sem.at[5 + hh]) for hh in range(per)]
    for load in loads[:3]:
        load.start()

    barrier = pltpu.get_barrier_semaphore()
    others = [at_x(1), at_x(2), at_x(3), at_y(1), at_y(2), at_y(3), at_zl, at_core, at_zh]
    for other in others:
        pl.semaphore_signal(barrier, inc=1, device_id=other, device_id_type=MESH)
    for load in loads[3:]:
        load.start()

    low = lax.broadcasted_iota(jnp.int32, (64, 128), 1) < DH
    lows = jnp.where(low, 1.0, 0.0).astype(BF16)
    highs = jnp.where(low, 0.0, 1.0).astype(BF16)
    stores = []

    def project(w, first, dst, factor=None, row=0, pairs=rows // 128):
        @pl.loop(0, width // COLS)
        def _(n):
            at = pl.multiple_of(first + n * COLS, COLS)
            acc = jnp.dot(tok[row:row + pairs * 128], w[:, pl.ds(at, COLS)], preferred_element_type=F32)
            if factor is not None:
                acc = acc * factor
            for pair in range(COLS // 128):
                for m in range(pairs):
                    even = acc[m * 128:m * 128 + 64, pair * 128:pair * 128 + 128]
                    odd = pltpu.roll(acc[m * 128 + 64:m * 128 + 128, pair * 128:pair * 128 + 128], 64, 1)
                    head = n * (COLS // DH) + 2 * pair
                    dst[head, :, m * 128:m * 128 + 128] = jnp.where(low, even, odd).astype(BF16)
                    dst[head + 1, :, m * 128:m * 128 + 128] = jnp.where(low, odd, even).astype(BF16)

    mine = zl * 2 + c
    theirs = (1 - zl) * 2 + c
    kv = {"k": (k_mine, k_all, k_more), "v": (v_mine, v_all, v_more)}

    def columns(stage):
        return {2: (2, 0, width), 3: (2, 0, 512), 4: (2, 512, 256)}.get(stage, (stage, 0, width))

    def kv_send(kind, hh):
        src, dst, _ = kv[kind]
        dst[hh, mine, x] = src[per * x + hh]
        for k in (1, 3, 2):
            to = lax.rem(x + k, NX)
            send(kind + "x", hh, k, src.at[per * to + hh], dst.at[hh, mine, x], at_x(k))

    def kv_more(kind):
        arrived("t", 0, 0)
        _, dst, src = kv[kind]
        project(wkv, 0 if kind == "k" else half, src, row=rows, pairs=1)
        for hh in range(per):
            dst[hh, theirs, x, :, 0:MORE] = src[per * x + hh]
        for k in (2, 1, 3):
            to = lax.rem(x + k, NX)
            send(
                kind + "t", 0, k, src.at[pl.ds(per * to, per)],
                dst.at[pl.ds(0, per), theirs, x, :, pl.ds(0, MORE)], at_x(k),
            )

    def across(stage):
        hh, lo, n = columns(stage)
        first = max(lo, MORE)
        return hh, pl.ds(first, lo + n - first)

    def kv_own(kind, stage):
        src, dst, _ = kv[kind]
        hh, at = across(stage)
        send(kind + "z", stage, 0, src.at[per * x + hh, :, at], dst.at[hh, mine, x, :, at], at_zl)

    def kv_forward(kind, stage):
        _, dst, _ = kv[kind]
        hh, at = across(stage)
        for k in (1, 3, 2):
            arrived(kind + "x", hh, k)
            block = dst.at[hh, mine, lax.rem(x + NX - k, NX), :, at]
            send(kind + "z", stage, k, block, block, at_zl)
        hh, lo, n = columns(stage)
        blocks = dst.at[hh, mine, :, :, pl.ds(lo, n)]
        send(kind + "c", stage, 0, blocks, blocks, at_core)

    def kv_last(kind, stage):
        _, dst, _ = kv[kind]
        arrived(kind + "t", 0, 2, 1, 3)
        arrived(kind + "z", stage, 0, 1, 3, 2)
        hh, lo, n = columns(stage)
        blocks = dst.at[hh, theirs, :, :, pl.ds(lo, n)]
        send(kind + "c", stage, 1, blocks, blocks, at_core)
        arrived(kind + "c", stage, 0, 1)

    def q_send(hh):
        q_all[hh, x] = q_mine[per * x + hh]
        for k in (2, 1, 3):
            to = lax.rem(x + k, NX)
            send("q", hh, k, q_mine.at[per * to + hh], q_all.at[hh, x], at_x(k))

    def logits(hh, half):
        arrived("q", hh, 2, 1, 3)

        @pl.loop(0, 2)
        def _(t):
            s = lax.dot_general(
                q_all[hh].reshape(256, width), k_all[hh, half * 2 + t].reshape(256, width),
                (((1,), (1,)), ((), ())), preferred_element_type=F32,
            ).reshape(NX, 64, 256)
            at = pl.ds(pl.multiple_of(t * 256, 256), 256)
            scores[:, :, at] = s
            part_out[hh, half, :, :, at] = s.astype(BF16)

        own_rows[hh, half] = scores[y]

    def send_rows(kind, hh, half):
        for k in (2, 1, 3):
            send(kind, hh, k, part_out.at[hh, half, lax.rem(y + k, NY)], part_in.at[hh, half, k - 1], at_y(k))

    def logits_mine(hh):
        arrived("kc", hh, 0)
        logits(hh, zl)
        send_rows("s", hh, zl)

    def logits_theirs(hh):
        logits(hh, 1 - zl)
        send_rows("r", hh, 1 - zl)

    def add_rows(hh):
        arrived("s", hh, 2, 1, 3)
        arrived("r", hh, 2, 1, 3)
        for half in range(2):
            total = own_rows[hh, half]
            for k in range(3):
                total = total + part_in[hh, half, k].astype(F32)
            own_rows[hh, half] = total
            pair_out[hh, half] = total.astype(BF16)
        send("p", hh, 0, pair_out.at[hh], pair_in.at[hh], at_zh)

    def softmax(hh):
        arrived("p", hh, 0)
        totals = [own_rows[hh, half] + pair_in[hh, half].astype(F32) for half in range(2)]
        largest = jnp.max(jnp.maximum(totals[0], totals[1]), axis=-1, keepdims=True)
        weights = [jnp.exp(total - largest) for total in totals]
        scaling = 1.0 / jnp.sum(weights[0] + weights[1], axis=-1, keepdims=True)
        for half in range(2):
            probs[hh, y, :, half * 512:half * 512 + 512] = (weights[half] * scaling).astype(BF16)
        for k in (1, 3):
            send("a", hh, k, probs.at[hh, y], probs.at[hh, y], at_y(k))

    def forward_probs(hh):
        for k, first in ((1, 0), (3, 32)):
            arrived("a", hh, k)
            block = probs.at[hh, lax.rem(y + NY - k, NY), pl.ds(first, 32)]
            send("b", hh, k, block, block, at_y(k))

    def attend(stage):
        hh, lo, n = columns(stage)
        arrived("a", hh, 1, 3)
        arrived("b", hh, 1, 3)

        @pl.loop(lo // COLS, (lo + n) // COLS)
        def _(tile):
            at = pl.ds(pl.multiple_of(tile * COLS, COLS), COLS)
            o = jnp.dot(
                probs[hh].reshape(256, 1024), v_all[hh, :, :, :, at].reshape(1024, COLS),
                preferred_element_type=F32,
            )
            att_out[hh, :, :, at] = o.astype(BF16).reshape(NX, 64, COLS)

        at = pl.ds(lo, n)
        att_all[per * x + hh, :, at] = att_out[hh, x, :, at]
        for k in (2, 1, 3):
            to = lax.rem(x + k, NX)
            send("o", stage, k, att_out.at[hh, to, :, at], att_all.at[per * x + hh, :, at], at_x(k))

    def swap_weights():
        for load in loads[5:]:
            load.wait()
        for hh in range(per):
            for xp in range(NX):
                wout[1, hh, xp] = wout[0, hh, xp ^ 1]

    def project_out(stage):
        hh, lo, n = columns(stage)
        arrived("o", stage, 2, 1, 3)
        m0, m1 = lo // 128, (lo + n) // 128
        for m in range(m0, m1):
            for pair in range(NX // 2):
                a = att_all[2 * pair * per + hh, :, m * 128:m * 128 + 128]
                b = att_all[(2 * pair + 1) * per + hh, :, m * 128:m * 128 + 128]
                left[0, m, :, pair * 128:pair * 128 + 128] = a * lows + b * highs
                left[1, m, :, pair * 128:pair * 128 + 128] = b * lows + a * highs

        @pl.loop(0, width // COLS)
        def _(tile):
            at = pl.ds(pl.multiple_of(tile * COLS, COLS), COLS)
            for q in range(2):
                s = (hh + q) % 2
                o = jnp.dot(
                    left[q, m0:m1].reshape((m1 - m0) * 64, NX * DH), wout[q, hh, :, :, at].reshape(NX * DH, COLS),
                    preferred_element_type=F32,
                ).reshape(m1 - m0, 64, COLS)
                mixed[s, m0:m1, :, at] = o if hh == 0 else mixed[s, m0:m1, :, at] + o
        if hh == per - 1:
            for s in range(2):
                copy = pltpu.make_async_copy(
                    mixed.at[s, pl.ds(m0, m1 - m0)], out_hbm.at[pl.ds(m0, m1 - m0), s],
                    load_sem.at[5 + 2 * stage + s],
                )
                copy.start()
                stores.append(copy)

    def start_tokens():
        loads[0].wait()
        pl.semaphore_wait(barrier, len(others))
        send("t", 0, 0, tok.at[pl.ds(0, 128)], tok.at[pl.ds(rows, 128)], at_zl)

    def project_keys():
        loads[1].wait()
        loads[2].wait()
        project(wkv, 0, k_mine)

    def project_query():
        loads[3].wait()
        project(wq, 0, q_mine, scale)

    def project_values():
        loads[4].wait()
        project(wkv, half, v_mine)

    start_tokens()
    project_keys()
    kv_send("k", 0)
    project_values()
    kv_own("k", 0)
    kv_send("k", 1)
    project_query()
    kv_own("k", 1)
    q_send(0)
    kv_forward("k", 0)
    kv_more("k")
    kv_forward("k", 1)
    kv_own("v", 0)
    kv_own("k", 2)
    q_send(1)
    kv_send("k", 2)
    logits_mine(0)
    kv_own("v", 1)
    kv_last("k", 0)
    logits_theirs(0)
    kv_last("k", 1)
    kv_own("v", 3)
    q_send(2)
    logits_mine(1)
    logits_theirs(1)
    kv_forward("k", 2)
    add_rows(0)
    kv_send("v", 0)
    kv_more("v")
    kv_send("v", 1)
    swap_weights()
    logits_mine(2)
    add_rows(1)
    kv_last("k", 2)
    logits_theirs(2)
    softmax(0)
    kv_forward("v", 0)
    kv_send("v", 2)
    softmax(1)
    add_rows(2)
    kv_forward("v", 1)
    forward_probs(0)
    kv_forward("v", 3)
    softmax(2)
    kv_own("v", 4)
    kv_last("v", 0)
    forward_probs(1)
    kv_forward("v", 4)
    attend(0)
    kv_last("v", 1)
    forward_probs(2)
    attend(1)
    kv_last("v", 3)
    attend(3)
    kv_last("v", 4)
    attend(4)
    project_out(0)
    project_out(1)
    project_out(3)
    project_out(4)

    for copy in copies.values():
        copy.wait_send()
    for copy in stores:
        copy.wait()


def local(tokens, w_query, w_keyval, w_out):
    seq_dev, res_dev, width = tokens.shape
    heads = width // DH
    per = heads // NX
    scale = 1.0 / math.sqrt(DH * seq_dev * lax.axis_size("seq"))
    rows = seq_dev * res_dev
    block = (heads, res_dev, seq_dev * DH)
    mixed = pl.pallas_call(
        functools.partial(layer_kernel, scale),
        out_shape=jax.ShapeDtypeStruct((seq_dev // 2, 2, res_dev, width), F32),
        in_specs=[pl.BlockSpec(memory_space=pltpu.HBM)] * 4,
        out_specs=pl.BlockSpec(memory_space=pl.ANY),
        scratch_shapes=[
            pltpu.VMEM((rows + 128, width), BF16),
            pltpu.VMEM((width, width), BF16),
            pltpu.VMEM((width, 2 * width), BF16),
            pltpu.VMEM((2, per, NX, DH, width), BF16),
            pltpu.VMEM(block, BF16),
            pltpu.VMEM(block, BF16),
            pltpu.VMEM(block, BF16),
            pltpu.VMEM((heads, res_dev, MORE), BF16),
            pltpu.VMEM((heads, res_dev, MORE), BF16),
            pltpu.VMEM((per, NX, res_dev, seq_dev * DH), BF16),
            pltpu.VMEM((per, 4, NX, res_dev, seq_dev * DH), BF16),
            pltpu.VMEM((per, 4, NX, res_dev, seq_dev * DH), BF16),
            pltpu.VMEM((NX, res_dev, 512), F32),
            pltpu.VMEM((per, 2, NY, res_dev, 512), BF16),
            pltpu.VMEM((per, 2, 3, res_dev, 512), BF16),
            pltpu.VMEM((per, 2, res_dev, 512), F32),
            pltpu.VMEM((per, 2, res_dev, 512), BF16),
            pltpu.VMEM((per, 2, res_dev, 512), BF16),
            pltpu.VMEM((per, NY, res_dev, 1024), BF16),
            pltpu.VMEM((per, NX, res_dev, seq_dev * DH), BF16),
            pltpu.VMEM(block, BF16),
            pltpu.VMEM((2, seq_dev // 2, res_dev, NX * DH), BF16),
            pltpu.VMEM((2, seq_dev // 2, res_dev, width), F32),
            pltpu.SemaphoreType.DMA((15,)),
            pltpu.SemaphoreType.DMA((16, 5, 4)),
            pltpu.SemaphoreType.DMA((16, 5, 4)),
        ],
        cost_estimate=pl.CostEstimate(flops=6 * 10**9, bytes_accessed=10**7, transcendentals=2 * 10**5),
        compiler_params=pltpu.CompilerParams(
            collective_id=0, has_side_effects=True, vmem_limit_bytes=44 * 2**20
        ),
        name="tied_row_attention",
    )(*[pltpu.with_memory_space_constraint(a, pltpu.HBM) for a in (tokens.reshape(rows, width), w_query, w_keyval, w_out.reshape(NX, per, DH, width))])
    return mixed.reshape(seq_dev, res_dev, width)


def solution(mesh):
    return jax.shard_map(
        local,
        mesh=mesh,
        in_specs=(P("seq", "res", None), P(), P(), P()),
        out_specs=P("seq", "res", None),
        check_vma=False,
    )
```

```python
import functools
import math

import jax
import jax.numpy as jnp
from jax import lax
from jax.experimental import pallas as pl
from jax.experimental.pallas import tpu as pltpu
from jax.sharding import PartitionSpec as P

DH = 64
NX, NY = 4, 4
COLS = 256
MORE = 128
MESH = pl.DeviceIdType.MESH
BF16, F32 = jnp.bfloat16, jnp.float32


def layer_kernel(
    scale,
    tok_hbm, wq_hbm, wkv_hbm, wout_ref, out_ref,
    tok, wq, wkv, wout, q_mine, k_mine, v_mine, k_more, v_more, q_all, k_all, v_all,
    scores, part_out, part_in, own_rows, pair_out, pair_in, probs, att_out, att_all, left,
    load_sem, send_sem, recv_sem,
):
    seq, res = lax.axis_index("seq"), lax.axis_index("res")
    y, zh = lax.div(seq, 2), lax.rem(seq, 2)
    zl, x, c = lax.div(res, 8), lax.rem(lax.div(res, 2), NX), lax.rem(res, 2)
    rows, width = tok_hbm.shape
    heads = q_mine.shape[0]
    per = heads // NX

    def at_x(k):
        return (seq, zl * 8 + lax.rem(x + k, NX) * 2 + c)

    def at_y(k):
        return (lax.rem(y + k, NY) * 2 + zh, res)

    at_zl = (seq, (1 - zl) * 8 + x * 2 + c)
    at_core = (seq, zl * 8 + x * 2 + (1 - c))
    at_zh = (y * 2 + (1 - zh), res)

    copies = {}
    seen = set()
    slots = ["kx", "kz", "kc", "kt", "vx", "vz", "vc", "vt", "q", "r", "s", "p", "u", "a", "e", "b", "o", "t"]

    def send(kind, stage, k, src, dst, where, when=None):
        slot = slots.index(kind)
        copy = pltpu.make_async_remote_copy(
            src_ref=src, dst_ref=dst,
            send_sem=send_sem.at[slot, stage, k], recv_sem=recv_sem.at[slot, stage, k],
            device_id=where, device_id_type=MESH,
        )
        if when is None:
            copy.start()
        else:
            pl.when(when)(copy.start)
        copies[kind, stage, k] = copy

    def arrived(kind, stage, *ks):
        for k in ks:
            if (kind, stage, k) not in seen:
                seen.add((kind, stage, k))
                copies[kind, stage, k].wait_recv()

    half = wkv.shape[1] // 2
    loads = [
        pltpu.make_async_copy(tok_hbm.at[pl.ds(0, 128)], tok.at[pl.ds(0, 128)], load_sem.at[0]),
        pltpu.make_async_copy(tok_hbm.at[pl.ds(128, rows - 128)], tok.at[pl.ds(128, rows - 128)], load_sem.at[1]),
        pltpu.make_async_copy(wkv_hbm.at[:, pl.ds(0, half)], wkv.at[:, pl.ds(0, half)], load_sem.at[2]),
        pltpu.make_async_copy(wq_hbm, wq, load_sem.at[3]),
        pltpu.make_async_copy(wkv_hbm.at[:, pl.ds(half, half)], wkv.at[:, pl.ds(half, half)], load_sem.at[4]),
    ] + [pltpu.make_async_copy(wout_ref.at[:, hh], wout.at[0, hh], load_sem.at[5 + hh]) for hh in range(per)]
    for load in loads[:3]:
        load.start()

    barrier = pltpu.get_barrier_semaphore()
    others = [at_x(1), at_x(2), at_x(3), at_y(1), at_y(2), at_y(3), at_zl, at_core, at_zh]
    for other in others:
        pl.semaphore_signal(barrier, inc=1, device_id=other, device_id_type=MESH)
    for load in loads[3:]:
        load.start()

    low = lax.broadcasted_iota(jnp.int32, (64, 128), 1) < DH
    lows = jnp.where(low, 1.0, 0.0).astype(BF16)
    highs = jnp.where(low, 0.0, 1.0).astype(BF16)

    def project(w, first, dst, factor=None, row=0, pairs=rows // 128, after=None):
        def tile(n):
            at = first + n * COLS if after else pl.multiple_of(first + n * COLS, COLS)
            acc = jnp.dot(tok[row:row + pairs * 128], w[:, pl.ds(at, COLS)], preferred_element_type=F32)
            if factor is not None:
                acc = acc * factor
            for pair in range(COLS // 128):
                for m in range(pairs):
                    even = acc[m * 128:m * 128 + 64, pair * 128:pair * 128 + 128]
                    odd = pltpu.roll(acc[m * 128 + 64:m * 128 + 128, pair * 128:pair * 128 + 128], 64, 1)
                    head = n * (COLS // DH) + 2 * pair
                    dst[head, :, m * 128:m * 128 + 128] = jnp.where(low, even, odd).astype(BF16)
                    dst[head + 1, :, m * 128:m * 128 + 128] = jnp.where(low, odd, even).astype(BF16)

        if after is None:
            pl.loop(0, width // COLS)(tile)
        else:
            for n in range(width // COLS):
                tile(n)
                after(n)

    mine = zl * 2 + c
    theirs = (1 - zl) * 2 + c
    kv = {"k": (k_mine, k_all, k_more), "v": (v_mine, v_all, v_more)}

    def columns(stage):
        return {2: (2, 0, width), 3: (2, 0, 512), 4: (2, 512, 256)}.get(stage, (stage, 0, width))

    def kv_send(kind, hh):
        src, dst, _ = kv[kind]
        dst[hh, mine, x] = src[per * x + hh]
        for k in (1, 3, 2):
            to = lax.rem(x + k, NX)
            send(kind + "x", hh, k, src.at[per * to + hh], dst.at[hh, mine, x], at_x(k))

    def kv_more(kind):
        arrived("t", 0, 0)
        _, dst, src = kv[kind]
        project(wkv, 0 if kind == "k" else half, src, row=rows, pairs=1)
        for hh in range(per):
            dst[hh, theirs, x, :, 0:MORE] = src[per * x + hh]
        for k in (2, 1, 3):
            to = lax.rem(x + k, NX)
            send(
                kind + "t", 0, k, src.at[pl.ds(per * to, per)],
                dst.at[pl.ds(0, per), theirs, x, :, pl.ds(0, MORE)], at_x(k),
            )

    def across(stage):
        hh, lo, n = columns(stage)
        first = max(lo, MORE)
        return hh, pl.ds(first, lo + n - first)

    def kv_own(kind, stage):
        src, dst, _ = kv[kind]
        hh, at = across(stage)
        send(kind + "z", stage, 0, src.at[per * x + hh, :, at], dst.at[hh, mine, x, :, at], at_zl)

    def kv_forward(kind, stage):
        _, dst, _ = kv[kind]
        hh, at = across(stage)
        for k in (1, 3, 2):
            arrived(kind + "x", hh, k)
            block = dst.at[hh, mine, lax.rem(x + NX - k, NX), :, at]
            send(kind + "z", stage, k, block, block, at_zl)
        hh, lo, n = columns(stage)
        blocks = dst.at[hh, mine, :, :, pl.ds(lo, n)]
        send(kind + "c", stage, 0, blocks, blocks, at_core)

    def kv_last(kind, stage):
        _, dst, _ = kv[kind]
        arrived(kind + "t", 0, 2, 1, 3)
        arrived(kind + "z", stage, 0, 1, 3, 2)
        hh, lo, n = columns(stage)
        blocks = dst.at[hh, theirs, :, :, pl.ds(lo, n)]
        send(kind + "c", stage, 1, blocks, blocks, at_core)
        arrived(kind + "c", stage, 0, 1)

    def q_send(hh):
        q_all[hh, x] = q_mine[per * x + hh]
        for k in (2, 1, 3):
            to = lax.rem(x + k, NX)
            send("q", hh, k, q_mine.at[per * to + hh], q_all.at[hh, x], at_x(k))

    def logits(hh, half):
        arrived("q", hh, 2, 1, 3)

        @pl.loop(0, 2)
        def _(t):
            s = lax.dot_general(
                q_all[hh].reshape(256, width), k_all[hh, half * 2 + t].reshape(256, width),
                (((1,), (1,)), ((), ())), preferred_element_type=F32,
            ).reshape(NX, 64, 256)
            at = pl.ds(pl.multiple_of(t * 256, 256), 256)
            scores[:, :, at] = s
            part_out[hh, half, :, :, at] = s.astype(BF16)

        own_rows[hh, half] = scores[y]

    def send_rows(kind, hh, half):
        for k in (2, 1, 3):
            send(kind, hh, k, part_out.at[hh, half, lax.rem(y + k, NY)], part_in.at[hh, half, k - 1], at_y(k))

    def logits_mine(hh):
        arrived("kc", hh, 0)
        logits(hh, zl)
        send_rows("s", hh, zl)

    def logits_theirs(hh):
        logits(hh, 1 - zl)
        send_rows("r", hh, 1 - zl)

    def add_rows(hh, kind, half, out):
        arrived(kind, hh, 2, 1, 3)
        total = own_rows[hh, half]
        for k in range(3):
            total = total + part_in[hh, half, k].astype(F32)
        own_rows[hh, half] = total
        pair_out[hh, half] = total.astype(BF16)
        send(out, hh, 0, pair_out.at[hh, half], pair_in.at[hh, half], at_zh)

    def add_mine(hh):
        add_rows(hh, "s", zl, "p")

    def add_theirs(hh):
        add_rows(hh, "r", 1 - zl, "u")

    def softmax(hh):
        arrived("p", hh, 0)
        arrived("u", hh, 0)
        totals = [own_rows[hh, half] + pair_in[hh, half].astype(F32) for half in range(2)]
        largest = jnp.max(jnp.maximum(totals[0], totals[1]), axis=-1, keepdims=True)
        weights = [jnp.exp(total - largest) for total in totals]
        scaling = 1.0 / jnp.sum(weights[0] + weights[1], axis=-1, keepdims=True)
        for half in range(2):
            probs[hh, y, :, half * 512:half * 512 + 512] = (weights[half] * scaling).astype(BF16)
        for kind, first in (("a", 0), ("e", 32)):
            for k in (1, 3):
                block = probs.at[hh, y, pl.ds(first if k == 1 else 32 - first, 32)]
                send(kind, hh, k, block, block, at_y(k))

    def forward_probs(hh):
        for k, first in ((1, 0), (3, 32)):
            arrived("a", hh, k)
            block = probs.at[hh, lax.rem(y + NY - k, NY), pl.ds(first, 32)]
            send("b", hh, k, block, block, at_y(k))

    def attend(stage):
        hh, lo, n = columns(stage)
        arrived("a", hh, 1, 3)
        arrived("e", hh, 1, 3)
        arrived("b", hh, 1, 3)

        @pl.loop(lo // COLS, (lo + n) // COLS)
        def _(tile):
            at = pl.ds(pl.multiple_of(tile * COLS, COLS), COLS)
            o = jnp.dot(
                probs[hh].reshape(256, 1024), v_all[hh, :, :, :, at].reshape(1024, COLS),
                preferred_element_type=F32,
            )
            att_out[hh, :, :, at] = o.astype(BF16).reshape(NX, 64, COLS)

        at = pl.ds(lo, n)
        att_all[per * x + hh, :, at] = att_out[hh, x, :, at]
        for k in (2, 1, 3):
            to = lax.rem(x + k, NX)
            send("o", stage, k, att_out.at[hh, to, :, at], att_all.at[per * x + hh, :, at], at_x(k))

    def swap_weights():
        for load in loads[5:]:
            load.wait()
        for hh in range(per):
            for xp in range(NX):
                wout[1, hh, xp] = wout[0, hh, xp ^ 1]

    def project_out(stage):
        hh, lo, n = columns(stage)
        arrived("o", stage, 2, 1, 3)
        m0, m1 = lo // 128, (lo + n) // 128
        for m in range(m0, m1):
            for pair in range(NX // 2):
                a = att_all[2 * pair * per + hh, :, m * 128:m * 128 + 128]
                b = att_all[(2 * pair + 1) * per + hh, :, m * 128:m * 128 + 128]
                left[0, m, :, pair * 128:pair * 128 + 128] = a * lows + b * highs
                left[1, m, :, pair * 128:pair * 128 + 128] = b * lows + a * highs

        @pl.loop(0, width // COLS)
        def _(tile):
            at = pl.ds(pl.multiple_of(tile * COLS, COLS), COLS)
            for q in range(2):
                s = (hh + q) % 2
                o = jnp.dot(
                    left[q, m0:m1].reshape((m1 - m0) * 64, NX * DH), wout[q, hh, :, :, at].reshape(NX * DH, COLS),
                    preferred_element_type=F32,
                ).reshape(m1 - m0, 64, COLS)
                out_ref[m0:m1, s, :, at] = o if hh == 0 else out_ref[m0:m1, s, :, at] + o

    sent = set()

    def drain(kinds=None, stages=range(5)):
        for key, copy in copies.items():
            if key not in sent and (kinds is None or key[0] in kinds) and key[1] in stages:
                sent.add(key)
                copy.wait_send()

    def drain_keys():
        drain(("t", "kx", "kz", "kc", "kt", "q", "r", "s"))

    def drain_most():
        drain(("vx", "vt", "p", "u"))
        drain(("vz", "vc", "a", "e", "b", "o"), (0,))

    def start_tokens():
        loads[0].wait()
        pl.semaphore_wait(barrier, len(others))
        send("t", 0, 0, tok.at[pl.ds(0, 128)], tok.at[pl.ds(rows, 128)], at_zl)

    def project_keys():
        loads[1].wait()
        loads[2].wait()
        src, dst, _ = kv["k"]

        def after(n):
            for k in (1, 3, 2):
                to = lax.rem(x + k, NX)
                ready = lax.div(per * to, COLS // DH) == n
                send("kx", 0, k, src.at[per * to], dst.at[0, mine, x], at_x(k), ready)

        project(wkv, 0, k_mine, after=after)
        dst[0, mine, x] = src[per * x]

    def project_query():
        loads[3].wait()
        project(wq, 0, q_mine, scale)

    def project_values():
        loads[4].wait()
        project(wkv, half, v_mine)

    start_tokens()
    project_keys()
    kv_own("k", 1)
    kv_send("k", 1)
    kv_more("k")
    kv_forward("k", 0)
    project_query()
    q_send(0)
    q_send(1)
    project_values()
    kv_own("k", 0)
    kv_forward("k", 1)
    kv_own("v", 0)
    kv_send("k", 2)
    kv_own("k", 2)
    q_send(2)
    kv_send("v", 0)
    kv_own("v", 4)
    kv_own("v", 1)
    kv_last("k", 0)
    logits_mine(0)
    logits_theirs(0)
    kv_last("k", 1)
    logits_mine(1)
    kv_send("v", 1)
    kv_forward("k", 2)
    logits_theirs(1)
    kv_more("v")
    kv_send("v", 2)
    add_mine(0)
    add_theirs(0)
    logits_mine(2)
    add_mine(1)
    add_theirs(1)
    kv_last("k", 2)
    logits_theirs(2)
    kv_forward("v", 0)
    softmax(0)
    softmax(1)
    add_mine(2)
    add_theirs(2)
    kv_forward("v", 1)
    kv_own("v", 3)
    forward_probs(0)
    drain_keys()
    kv_last("v", 0)
    forward_probs(1)
    softmax(2)
    kv_forward("v", 3)
    attend(0)
    swap_weights()
    kv_forward("v", 4)
    kv_last("v", 1)
    attend(1)
    forward_probs(2)
    drain_most()
    kv_last("v", 3)
    attend(3)
    kv_last("v", 4)
    attend(4)
    project_out(0)
    project_out(1)
    project_out(3)
    project_out(4)

    drain()


def local(tokens, w_query, w_keyval, w_out):
    seq_dev, res_dev, width = tokens.shape
    heads = width // DH
    per = heads // NX
    scale = 1.0 / math.sqrt(DH * seq_dev * lax.axis_size("seq"))
    rows = seq_dev * res_dev
    block = (heads, res_dev, seq_dev * DH)
    mixed = pl.pallas_call(
        functools.partial(layer_kernel, scale),
        out_shape=jax.ShapeDtypeStruct((seq_dev // 2, 2, res_dev, width), F32),
        in_specs=[pl.BlockSpec(memory_space=pltpu.HBM)] * 4,
        out_specs=pl.BlockSpec(memory_space=pltpu.VMEM),
        scratch_shapes=[
            pltpu.VMEM((rows + 128, width), BF16),
            pltpu.VMEM((width, width), BF16),
            pltpu.VMEM((width, 2 * width), BF16),
            pltpu.VMEM((2, per, NX, DH, width), BF16),
            pltpu.VMEM(block, BF16),
            pltpu.VMEM(block, BF16),
            pltpu.VMEM(block, BF16),
            pltpu.VMEM((heads, res_dev, MORE), BF16),
            pltpu.VMEM((heads, res_dev, MORE), BF16),
            pltpu.VMEM((per, NX, res_dev, seq_dev * DH), BF16),
            pltpu.VMEM((per, 4, NX, res_dev, seq_dev * DH), BF16),
            pltpu.VMEM((per, 4, NX, res_dev, seq_dev * DH), BF16),
            pltpu.VMEM((NX, res_dev, 512), F32),
            pltpu.VMEM((per, 2, NY, res_dev, 512), BF16),
            pltpu.VMEM((per, 2, 3, res_dev, 512), BF16),
            pltpu.VMEM((per, 2, res_dev, 512), F32),
            pltpu.VMEM((per, 2, res_dev, 512), BF16),
            pltpu.VMEM((per, 2, res_dev, 512), BF16),
            pltpu.VMEM((per, NY, res_dev, 1024), BF16),
            pltpu.VMEM((per, NX, res_dev, seq_dev * DH), BF16),
            pltpu.VMEM(block, BF16),
            pltpu.VMEM((2, seq_dev // 2, res_dev, NX * DH), BF16),
            pltpu.SemaphoreType.DMA((8,)),
            pltpu.SemaphoreType.DMA((18, 5, 4)),
            pltpu.SemaphoreType.DMA((18, 5, 4)),
        ],
        cost_estimate=pl.CostEstimate(flops=6 * 10**9, bytes_accessed=10**7, transcendentals=2 * 10**5),
        compiler_params=pltpu.CompilerParams(
            collective_id=0, has_side_effects=True, vmem_limit_bytes=44 * 2**20
        ),
        name="tied_row_attention",
    )(*[pltpu.with_memory_space_constraint(a, pltpu.HBM) for a in (tokens.reshape(rows, width), w_query, w_keyval, w_out.reshape(NX, per, DH, width))])
    return mixed.reshape(seq_dev, res_dev, width)


def solution(mesh):
    return jax.shard_map(
        local,
        mesh=mesh,
        in_specs=(P("seq", "res", None), P(), P(), P()),
        out_specs=P("seq", "res", None),
        check_vma=False,
    )
```

```python
import functools
import math

import jax
import jax.numpy as jnp
from jax import lax
from jax.experimental import pallas as pl
from jax.experimental.pallas import tpu as pltpu
from jax.sharding import PartitionSpec as P

DH = 64
NX, NY = 4, 4
COLS = 256
MORE = 128
MESH = pl.DeviceIdType.MESH
BF16, F32 = jnp.bfloat16, jnp.float32


def layer_kernel(
    scale,
    tok_hbm, wq_hbm, wkv_hbm, wout_ref, out_ref,
    tok, wq, wkv, wout, q_mine, k_mine, v_mine, k_more, v_more, q_all, k_all, v_all,
    scores, part_out, part_in, own_rows, pair_out, pair_in, probs, att_out, att_all, left,
    load_sem, send_sem, recv_sem,
):
    seq, res = lax.axis_index("seq"), lax.axis_index("res")
    y, zh = lax.div(seq, 2), lax.rem(seq, 2)
    zl, x, c = lax.div(res, 8), lax.rem(lax.div(res, 2), NX), lax.rem(res, 2)
    rows, width = tok_hbm.shape
    heads = q_mine.shape[0]
    per = heads // NX

    def at_x(k):
        return (seq, zl * 8 + lax.rem(x + k, NX) * 2 + c)

    def at_y(k):
        return (lax.rem(y + k, NY) * 2 + zh, res)

    at_zl = (seq, (1 - zl) * 8 + x * 2 + c)
    at_core = (seq, zl * 8 + x * 2 + (1 - c))
    at_zh = (y * 2 + (1 - zh), res)

    copies = {}
    seen = set()
    numbers = {}

    def send(kind, stage, k, src, dst, where, when=None):
        number = numbers.setdefault((kind, stage, k), len(numbers))
        copy = pltpu.make_async_remote_copy(
            src_ref=src, dst_ref=dst,
            send_sem=send_sem.at[number], recv_sem=recv_sem.at[number],
            device_id=where, device_id_type=MESH,
        )
        if when is None:
            copy.start()
        else:
            pl.when(when)(copy.start)
        copies[kind, stage, k] = copy

    def arrived(kind, stage, *ks):
        for k in ks:
            if (kind, stage, k) not in seen:
                seen.add((kind, stage, k))
                copies[kind, stage, k].wait_recv()

    half = wkv.shape[1] // 2
    loads = [
        pltpu.make_async_copy(tok_hbm.at[pl.ds(0, 128)], tok.at[pl.ds(0, 128)], load_sem.at[0]),
        pltpu.make_async_copy(tok_hbm.at[pl.ds(128, rows - 128)], tok.at[pl.ds(128, rows - 128)], load_sem.at[1]),
        pltpu.make_async_copy(wkv_hbm.at[:, pl.ds(0, half)], wkv.at[:, pl.ds(0, half)], load_sem.at[2]),
        pltpu.make_async_copy(wq_hbm, wq, load_sem.at[3]),
        pltpu.make_async_copy(wkv_hbm.at[:, pl.ds(half, half)], wkv.at[:, pl.ds(half, half)], load_sem.at[4]),
    ] + [pltpu.make_async_copy(wout_ref.at[:, hh], wout.at[0, hh], load_sem.at[5 + hh]) for hh in range(per)]
    for load in loads[:3]:
        load.start()

    barrier = pltpu.get_barrier_semaphore()
    others = [at_x(1), at_x(2), at_x(3), at_y(1), at_y(2), at_y(3), at_zl, at_core, at_zh]
    for other in others:
        pl.semaphore_signal(barrier, inc=1, device_id=other, device_id_type=MESH)
    for load in loads[3:]:
        load.start()

    low = lax.broadcasted_iota(jnp.int32, (64, 128), 1) < DH
    lows = jnp.where(low, 1.0, 0.0).astype(BF16)
    highs = jnp.where(low, 0.0, 1.0).astype(BF16)

    def project(w, first, dst, factor=None, row=0, pairs=rows // 128, after=None):
        def tile(n):
            at = first + n * COLS if after else pl.multiple_of(first + n * COLS, COLS)
            acc = jnp.dot(tok[row:row + pairs * 128], w[:, pl.ds(at, COLS)], preferred_element_type=F32)
            if factor is not None:
                acc = acc * factor
            for pair in range(COLS // 128):
                for m in range(pairs):
                    even = acc[m * 128:m * 128 + 64, pair * 128:pair * 128 + 128]
                    odd = pltpu.roll(acc[m * 128 + 64:m * 128 + 128, pair * 128:pair * 128 + 128], 64, 1)
                    head = n * (COLS // DH) + 2 * pair
                    dst[head, :, m * 128:m * 128 + 128] = jnp.where(low, even, odd).astype(BF16)
                    dst[head + 1, :, m * 128:m * 128 + 128] = jnp.where(low, odd, even).astype(BF16)

        if after is None:
            pl.loop(0, width // COLS)(tile)
        else:
            for n in range(width // COLS):
                tile(n)
                after(n)

    mine = zl * 2 + c
    theirs = (1 - zl) * 2 + c
    kv = {"k": (k_mine, k_all, k_more), "v": (v_mine, v_all, v_more)}

    def columns(stage):
        return {2: (2, 0, width), 3: (2, 0, 512), 4: (2, 512, 256)}.get(stage, (stage, 0, width))

    def kv_send(kind, hh):
        src, dst, _ = kv[kind]
        dst[hh, mine, x] = src[per * x + hh]
        for k in (1, 3, 2):
            to = lax.rem(x + k, NX)
            send(kind + "x", hh, k, src.at[per * to + hh], dst.at[hh, mine, x], at_x(k))

    def kv_more(kind):
        arrived("t", 0, 0)
        _, dst, src = kv[kind]
        project(wkv, 0 if kind == "k" else half, src, row=rows, pairs=1)
        for hh in range(per):
            dst[hh, theirs, x, :, 0:MORE] = src[per * x + hh]
        for k in (2, 1, 3):
            to = lax.rem(x + k, NX)
            send(
                kind + "t", 0, k, src.at[pl.ds(per * to, per)],
                dst.at[pl.ds(0, per), theirs, x, :, pl.ds(0, MORE)], at_x(k),
            )

    def across(stage):
        hh, lo, n = columns(stage)
        first = max(lo, MORE)
        return hh, pl.ds(first, lo + n - first)

    def kv_own(kind, stage):
        src, dst, _ = kv[kind]
        hh, at = across(stage)
        send(kind + "z", stage, 0, src.at[per * x + hh, :, at], dst.at[hh, mine, x, :, at], at_zl)

    def kv_forward(kind, stage):
        _, dst, _ = kv[kind]
        hh, at = across(stage)
        for k in (1, 3, 2):
            arrived(kind + "x", hh, k)
            block = dst.at[hh, mine, lax.rem(x + NX - k, NX), :, at]
            send(kind + "z", stage, k, block, block, at_zl)
        hh, lo, n = columns(stage)
        blocks = dst.at[hh, mine, :, :, pl.ds(lo, n)]
        send(kind + "c", stage, 0, blocks, blocks, at_core)

    def kv_last(kind, stage):
        _, dst, _ = kv[kind]
        arrived(kind + "t", 0, 2, 1, 3)
        arrived(kind + "z", stage, 0, 1, 3, 2)
        hh, lo, n = columns(stage)
        blocks = dst.at[hh, theirs, :, :, pl.ds(lo, n)]
        send(kind + "c", stage, 1, blocks, blocks, at_core)
        arrived(kind + "c", stage, 0, 1)

    def q_send(hh):
        q_all[hh, x] = q_mine[per * x + hh]
        for k in (2, 1, 3):
            to = lax.rem(x + k, NX)
            send("q", hh, k, q_mine.at[per * to + hh], q_all.at[hh, x], at_x(k))

    def logits(hh, half):
        arrived("q", hh, 2, 1, 3)

        @pl.loop(0, 2)
        def _(t):
            s = lax.dot_general(
                q_all[hh].reshape(256, width), k_all[hh, half * 2 + t].reshape(256, width),
                (((1,), (1,)), ((), ())), preferred_element_type=F32,
            ).reshape(NX, 64, 256)
            at = pl.ds(pl.multiple_of(t * 256, 256), 256)
            scores[:, :, at] = s
            part_out[hh, half, :, :, at] = s.astype(BF16)

        own_rows[hh, half] = scores[y]

    def send_rows(kind, hh, half):
        for k in (2, 1, 3):
            send(kind, hh, k, part_out.at[hh, half, lax.rem(y + k, NY)], part_in.at[hh, half, k - 1], at_y(k))

    def logits_mine(hh):
        arrived("kc", hh, 0)
        logits(hh, zl)
        send_rows("s", hh, zl)

    def logits_theirs(hh):
        logits(hh, 1 - zl)
        send_rows("r", hh, 1 - zl)

    def add_rows(hh, kind, half, out):
        arrived(kind, hh, 2, 1, 3)
        total = own_rows[hh, half]
        for k in range(3):
            total = total + part_in[hh, half, k].astype(F32)
        own_rows[hh, half] = total
        pair_out[hh, half] = total.astype(BF16)
        send(out, hh, 0, pair_out.at[hh, half], pair_in.at[hh, half], at_zh)

    def add_mine(hh):
        add_rows(hh, "s", zl, "p")

    def add_theirs(hh):
        add_rows(hh, "r", 1 - zl, "u")

    def softmax(hh):
        arrived("p", hh, 0)
        arrived("u", hh, 0)
        totals = [own_rows[hh, half] + pair_in[hh, half].astype(F32) for half in range(2)]
        largest = jnp.max(jnp.maximum(totals[0], totals[1]), axis=-1, keepdims=True)
        weights = [jnp.exp(total - largest) for total in totals]
        scaling = 1.0 / jnp.sum(weights[0] + weights[1], axis=-1, keepdims=True)
        for half in range(2):
            probs[hh, y, :, half * 512:half * 512 + 512] = (weights[half] * scaling).astype(BF16)
        for kind, first in (("a", 0), ("e", 32)):
            for k in (1, 3):
                block = probs.at[hh, y, pl.ds(first if k == 1 else 32 - first, 32)]
                send(kind, hh, k, block, block, at_y(k))

    def forward_probs(hh):
        for k, first in ((1, 0), (3, 32)):
            arrived("a", hh, k)
            block = probs.at[hh, lax.rem(y + NY - k, NY), pl.ds(first, 32)]
            send("b", hh, k, block, block, at_y(k))

    def attend(stage):
        hh, lo, n = columns(stage)
        arrived("a", hh, 1, 3)
        arrived("e", hh, 1, 3)
        arrived("b", hh, 1, 3)

        @pl.loop(lo // COLS, (lo + n) // COLS)
        def _(tile):
            at = pl.ds(pl.multiple_of(tile * COLS, COLS), COLS)
            o = jnp.dot(
                probs[hh].reshape(256, 1024), v_all[hh, :, :, :, at].reshape(1024, COLS),
                preferred_element_type=F32,
            )
            att_out[hh, :, :, at] = o.astype(BF16).reshape(NX, 64, COLS)

        at = pl.ds(lo, n)
        att_all[per * x + hh, :, at] = att_out[hh, x, :, at]
        for k in (2, 1, 3):
            to = lax.rem(x + k, NX)
            send("o", stage, k, att_out.at[hh, to, :, at], att_all.at[per * x + hh, :, at], at_x(k))

    def swap_weights():
        for load in loads[5:]:
            load.wait()
        for hh in range(per):
            for xp in range(NX):
                wout[1, hh, xp] = wout[0, hh, xp ^ 1]

    def project_out(stage):
        hh, lo, n = columns(stage)
        arrived("o", stage, 2, 1, 3)
        m0, m1 = lo // 128, (lo + n) // 128
        for m in range(m0, m1):
            for pair in range(NX // 2):
                a = att_all[2 * pair * per + hh, :, m * 128:m * 128 + 128]
                b = att_all[(2 * pair + 1) * per + hh, :, m * 128:m * 128 + 128]
                left[0, m, :, pair * 128:pair * 128 + 128] = a * lows + b * highs
                left[1, m, :, pair * 128:pair * 128 + 128] = b * lows + a * highs

        @pl.loop(0, width // COLS)
        def _(tile):
            at = pl.ds(pl.multiple_of(tile * COLS, COLS), COLS)
            for q in range(2):
                s = (hh + q) % 2
                o = jnp.dot(
                    left[q, m0:m1].reshape((m1 - m0) * 64, NX * DH), wout[q, hh, :, :, at].reshape(NX * DH, COLS),
                    preferred_element_type=F32,
                ).reshape(m1 - m0, 64, COLS)
                out_ref[m0:m1, s, :, at] = o if hh == 0 else out_ref[m0:m1, s, :, at] + o

    sent = set()

    def drain(kinds=None, stages=range(5)):
        for key, copy in copies.items():
            if key not in sent and (kinds is None or key[0] in kinds) and key[1] in stages:
                sent.add(key)
                copy.wait_send()

    def drain_keys():
        drain(("t", "kx", "kz", "kc", "kt", "q", "r", "s"))

    def drain_most():
        drain(("vx", "vt", "p", "u"))
        drain(("vz", "vc", "a", "e", "b", "o"), (0,))

    def start_tokens():
        loads[0].wait()
        pl.semaphore_wait(barrier, len(others))
        send("t", 0, 0, tok.at[pl.ds(0, 128)], tok.at[pl.ds(rows, 128)], at_zl)

    def project_keys():
        loads[1].wait()
        loads[2].wait()
        src, dst, _ = kv["k"]

        def after(n):
            for k in (1, 3, 2):
                to = lax.rem(x + k, NX)
                ready = lax.div(per * to, COLS // DH) == n
                send("kx", 0, k, src.at[per * to], dst.at[0, mine, x], at_x(k), ready)

        project(wkv, 0, k_mine, after=after)
        dst[0, mine, x] = src[per * x]

    def project_query():
        loads[3].wait()
        project(wq, 0, q_mine, scale)

    def project_values():
        loads[4].wait()
        project(wkv, half, v_mine)

    start_tokens()
    project_keys()
    kv_own("k", 1)
    kv_send("k", 1)
    kv_more("k")
    kv_forward("k", 0)
    project_query()
    q_send(0)
    q_send(1)
    project_values()
    kv_own("k", 0)
    kv_forward("k", 1)
    kv_own("v", 0)
    kv_send("k", 2)
    kv_own("k", 2)
    q_send(2)
    kv_send("v", 0)
    kv_own("v", 4)
    kv_own("v", 1)
    kv_last("k", 0)
    logits_mine(0)
    logits_theirs(0)
    kv_last("k", 1)
    logits_mine(1)
    kv_send("v", 1)
    kv_forward("k", 2)
    logits_theirs(1)
    kv_more("v")
    kv_send("v", 2)
    add_mine(0)
    add_theirs(0)
    logits_mine(2)
    add_mine(1)
    add_theirs(1)
    kv_last("k", 2)
    logits_theirs(2)
    kv_forward("v", 0)
    softmax(0)
    softmax(1)
    add_mine(2)
    add_theirs(2)
    kv_forward("v", 1)
    kv_own("v", 3)
    forward_probs(0)
    drain_keys()
    kv_last("v", 0)
    forward_probs(1)
    softmax(2)
    kv_forward("v", 3)
    attend(0)
    swap_weights()
    kv_forward("v", 4)
    kv_last("v", 1)
    attend(1)
    forward_probs(2)
    drain_most()
    kv_last("v", 3)
    attend(3)
    kv_last("v", 4)
    attend(4)
    project_out(0)
    project_out(1)
    project_out(3)
    project_out(4)

    drain()


def local(tokens, w_query, w_keyval, w_out):
    seq_dev, res_dev, width = tokens.shape
    heads = width // DH
    per = heads // NX
    scale = 1.0 / math.sqrt(DH * seq_dev * lax.axis_size("seq"))
    rows = seq_dev * res_dev
    block = (heads, res_dev, seq_dev * DH)
    mixed = pl.pallas_call(
        functools.partial(layer_kernel, scale),
        out_shape=jax.ShapeDtypeStruct((seq_dev // 2, 2, res_dev, width), F32),
        in_specs=[pl.BlockSpec(memory_space=pltpu.HBM)] * 4,
        out_specs=pl.BlockSpec(memory_space=pltpu.VMEM),
        scratch_shapes=[
            pltpu.VMEM((rows + 128, width), BF16),
            pltpu.VMEM((width, width), BF16),
            pltpu.VMEM((width, 2 * width), BF16),
            pltpu.VMEM((2, per, NX, DH, width), BF16),
            pltpu.VMEM(block, BF16),
            pltpu.VMEM(block, BF16),
            pltpu.VMEM(block, BF16),
            pltpu.VMEM((heads, res_dev, MORE), BF16),
            pltpu.VMEM((heads, res_dev, MORE), BF16),
            pltpu.VMEM((per, NX, res_dev, seq_dev * DH), BF16),
            pltpu.VMEM((per, 4, NX, res_dev, seq_dev * DH), BF16),
            pltpu.VMEM((per, 4, NX, res_dev, seq_dev * DH), BF16),
            pltpu.VMEM((NX, res_dev, 512), F32),
            pltpu.VMEM((per, 2, NY, res_dev, 512), BF16),
            pltpu.VMEM((per, 2, 3, res_dev, 512), BF16),
            pltpu.VMEM((per, 2, res_dev, 512), F32),
            pltpu.VMEM((per, 2, res_dev, 512), BF16),
            pltpu.VMEM((per, 2, res_dev, 512), BF16),
            pltpu.VMEM((per, NY, res_dev, 1024), BF16),
            pltpu.VMEM((per, NX, res_dev, seq_dev * DH), BF16),
            pltpu.VMEM(block, BF16),
            pltpu.VMEM((2, seq_dev // 2, res_dev, NX * DH), BF16),
            pltpu.SemaphoreType.DMA((8,)),
            pltpu.SemaphoreType.DMA((132,)),
            pltpu.SemaphoreType.DMA((132,)),
        ],
        cost_estimate=pl.CostEstimate(flops=6 * 10**9, bytes_accessed=10**7, transcendentals=2 * 10**5),
        compiler_params=pltpu.CompilerParams(
            collective_id=0, has_side_effects=True, vmem_limit_bytes=44 * 2**20
        ),
        name="tied_row_attention",
    )(*[pltpu.with_memory_space_constraint(a, pltpu.HBM) for a in (tokens.reshape(rows, width), w_query, w_keyval, w_out.reshape(NX, per, DH, width))])
    return mixed.reshape(seq_dev, res_dev, width)


def solution(mesh):
    return jax.shard_map(
        local,
        mesh=mesh,
        in_specs=(P("seq", "res", None), P(), P(), P()),
        out_specs=P("seq", "res", None),
        check_vma=False,
    )
```

```python
import functools
import math

import jax
import jax.numpy as jnp
from jax import lax
from jax.experimental import pallas as pl
from jax.experimental.pallas import tpu as pltpu
from jax.sharding import PartitionSpec as P

DH = 64
NX, NY = 4, 4
COLS = 256
MORE = 128
MESH = pl.DeviceIdType.MESH
BF16, F32 = jnp.bfloat16, jnp.float32


def layer_kernel(
    scale,
    tok_hbm, wq_hbm, wkv_hbm, wout_ref, out_ref,
    tok, wq, wkv, wout, q_mine, k_mine, v_mine, k_more, v_more, q_all, k_all, v_all,
    scores, part_out, part_in, own_rows, pair_out, pair_in, probs, att_out, att_all, lhs,
    load_sem, send_sem, recv_sem,
):
    seq, res = lax.axis_index("seq"), lax.axis_index("res")
    y, zh = lax.div(seq, 2), lax.rem(seq, 2)
    zl, x, c = lax.div(res, 8), lax.rem(lax.div(res, 2), NX), lax.rem(res, 2)
    rows, width = tok_hbm.shape
    heads = q_mine.shape[0]
    per = heads // NX

    def at_x(k):
        return (seq, zl * 8 + lax.rem(x + k, NX) * 2 + c)

    def at_y(k):
        return (lax.rem(y + k, NY) * 2 + zh, res)

    at_zl = (seq, (1 - zl) * 8 + x * 2 + c)
    at_core = (seq, zl * 8 + x * 2 + (1 - c))
    at_zh = (y * 2 + (1 - zh), res)

    senders, receivers, seen = {}, {}, set()

    def send(kind, group, src, dst, where, when=None):
        copy = pltpu.make_async_remote_copy(
            src_ref=src, dst_ref=dst,
            send_sem=send_sem.at[senders.setdefault(kind, len(senders))],
            recv_sem=recv_sem.at[receivers.setdefault(group, len(receivers))],
            device_id=where, device_id_type=MESH,
        )
        if when is None:
            copy.start()
        else:
            pl.when(when)(copy.start)

    def arrived(group, ref):
        if group not in seen:
            seen.add(group)
            pltpu.make_async_copy(ref, ref, recv_sem.at[receivers[group]]).wait()

    def left(kind, ref):
        pltpu.make_async_copy(ref, ref, send_sem.at[senders[kind]]).wait()

    half = wkv.shape[1] // 2
    loads = [
        pltpu.make_async_copy(tok_hbm.at[pl.ds(0, 128)], tok.at[pl.ds(0, 128)], load_sem.at[0]),
        pltpu.make_async_copy(tok_hbm.at[pl.ds(128, rows - 128)], tok.at[pl.ds(128, rows - 128)], load_sem.at[1]),
        pltpu.make_async_copy(wkv_hbm.at[:, pl.ds(0, half)], wkv.at[:, pl.ds(0, half)], load_sem.at[2]),
        pltpu.make_async_copy(wq_hbm, wq, load_sem.at[3]),
        pltpu.make_async_copy(wkv_hbm.at[:, pl.ds(half, half)], wkv.at[:, pl.ds(half, half)], load_sem.at[4]),
    ] + [pltpu.make_async_copy(wout_ref.at[:, hh], wout.at[0, hh], load_sem.at[5 + hh]) for hh in range(per)]
    for load in loads[:3]:
        load.start()

    barrier = pltpu.get_barrier_semaphore()
    others = [at_x(1), at_x(2), at_x(3), at_y(1), at_y(2), at_y(3), at_zl, at_core, at_zh]
    for other in others:
        pl.semaphore_signal(barrier, inc=1, device_id=other, device_id_type=MESH)
    for load in loads[3:]:
        load.start()

    low = lax.broadcasted_iota(jnp.int32, (64, 128), 1) < DH
    lows = jnp.where(low, 1.0, 0.0).astype(BF16)
    highs = jnp.where(low, 0.0, 1.0).astype(BF16)

    def project(w, first, dst, factor=None, row=0, pairs=rows // 128, after=None):
        def tile(n):
            at = first + n * COLS if after else pl.multiple_of(first + n * COLS, COLS)
            acc = jnp.dot(tok[row:row + pairs * 128], w[:, pl.ds(at, COLS)], preferred_element_type=F32)
            if factor is not None:
                acc = acc * factor
            for pair in range(COLS // 128):
                for m in range(pairs):
                    even = acc[m * 128:m * 128 + 64, pair * 128:pair * 128 + 128]
                    odd = pltpu.roll(acc[m * 128 + 64:m * 128 + 128, pair * 128:pair * 128 + 128], 64, 1)
                    head = n * (COLS // DH) + 2 * pair
                    dst[head, :, m * 128:m * 128 + 128] = jnp.where(low, even, odd).astype(BF16)
                    dst[head + 1, :, m * 128:m * 128 + 128] = jnp.where(low, odd, even).astype(BF16)

        if after is None:
            pl.loop(0, width // COLS)(tile)
        else:
            for n in range(width // COLS):
                tile(n)
                after(n)

    mine = zl * 2 + c
    theirs = (1 - zl) * 2 + c
    kv = {"k": (k_mine, k_all, k_more), "v": (v_mine, v_all, v_more)}

    def columns(stage):
        return {2: (2, 0, width), 3: (2, 0, 512), 4: (2, 512, 256)}.get(stage, (stage, 0, width))

    def kv_send(kind, hh):
        src, dst, _ = kv[kind]
        dst[hh, mine, x] = src[per * x + hh]
        for k in (1, 3, 2):
            to = lax.rem(x + k, NX)
            group = (kind + "x", hh, k if kind == "k" else 0)
            send(kind + "x", group, src.at[per * to + hh], dst.at[hh, mine, x], at_x(k))

    def kv_more(kind):
        arrived("t", tok.at[pl.ds(rows, 128)])
        _, dst, src = kv[kind]
        project(wkv, 0 if kind == "k" else half, src, row=rows, pairs=1)
        for hh in range(per):
            dst[hh, theirs, x, :, 0:MORE] = src[per * x + hh]
        for k in (2, 1, 3):
            to = lax.rem(x + k, NX)
            send(
                kind + "t", kind + "t", src.at[pl.ds(per * to, per)],
                dst.at[pl.ds(0, per), theirs, x, :, pl.ds(0, MORE)], at_x(k),
            )

    def across(stage):
        hh, lo, n = columns(stage)
        first = max(lo, MORE)
        return hh, pl.ds(first, lo + n - first)

    def kv_own(kind, stage):
        src, dst, _ = kv[kind]
        hh, at = across(stage)
        send(kind + "z", (kind + "z", stage), src.at[per * x + hh, :, at], dst.at[hh, mine, x, :, at], at_zl)

    def kv_forward(kind, stage):
        _, dst, _ = kv[kind]
        hh, at = across(stage)
        for k in (1, 3, 2):
            block = dst.at[hh, mine, lax.rem(x + NX - k, NX)]
            if kind == "k":
                arrived(("kx", hh, k), block)
            else:
                arrived(("vx", hh, 0), dst.at[hh, mine, pl.ds(0, 3)])
            block = block.at[:, at]
            send(kind + "z", (kind + "z", stage), block, block, at_zl)
        hh, lo, n = columns(stage)
        blocks = dst.at[hh, mine, :, :, pl.ds(lo, n)]
        send(kind + "c", (kind + "c", stage, 0), blocks, blocks, at_core)

    def kv_last(kind, stage):
        _, dst, _ = kv[kind]
        arrived(kind + "t", dst.at[pl.ds(0, per), theirs, pl.ds(0, 3), :, pl.ds(0, MORE)])
        hh, at = across(stage)
        arrived((kind + "z", stage), dst.at[hh, theirs, :, :, at])
        hh, lo, n = columns(stage)
        at = pl.ds(lo, n)
        blocks = dst.at[hh, theirs, :, :, at]
        if kind == "k":
            send("kc", ("kc", stage, 1), blocks, blocks, at_core)
            arrived(("kc", stage, 0), dst.at[hh, 2 * zl + 1 - c])
            arrived(("kc", stage, 1), dst.at[hh, 2 * (1 - zl) + 1 - c])
        else:
            send("vc", ("vc", stage, 0), blocks, blocks, at_core)
            arrived(("vc", stage, 0), dst.at[hh, pl.ds(0, 2), :, :, at])

    def q_send(hh):
        q_all[hh, x] = q_mine[per * x + hh]
        for k in (2, 1, 3):
            to = lax.rem(x + k, NX)
            send("q", ("q", hh), q_mine.at[per * to + hh], q_all.at[hh, x], at_x(k))

    def logits(hh, half):
        arrived(("q", hh), q_all.at[hh, pl.ds(0, 3)])

        @pl.loop(0, 2)
        def _(t):
            s = lax.dot_general(
                q_all[hh].reshape(256, width), k_all[hh, half * 2 + t].reshape(256, width),
                (((1,), (1,)), ((), ())), preferred_element_type=F32,
            ).reshape(NX, 64, 256)
            at = pl.ds(pl.multiple_of(t * 256, 256), 256)
            scores[:, :, at] = s
            part_out[hh, half, :, :, at] = s.astype(BF16)

        own_rows[hh, half] = scores[y]

    def send_rows(kind, hh, half):
        for k in (2, 1, 3):
            send(
                kind, (kind, hh), part_out.at[hh, half, lax.rem(y + k, NY)], part_in.at[hh, half, k - 1], at_y(k)
            )

    def logits_mine(hh):
        arrived(("kc", hh, 0), k_all.at[hh, 2 * zl + 1 - c])
        logits(hh, zl)
        send_rows("s", hh, zl)

    def logits_theirs(hh):
        logits(hh, 1 - zl)
        send_rows("r", hh, 1 - zl)

    def add_rows(hh, kind, half):
        arrived((kind, hh), part_in.at[hh, half])
        total = own_rows[hh, half]
        for k in range(3):
            total = total + part_in[hh, half, k].astype(F32)
        own_rows[hh, half] = total
        pair_out[hh, half] = total.astype(BF16)
        send("p", ("p", hh), pair_out.at[hh, half], pair_in.at[hh, half], at_zh)

    def add_mine(hh):
        add_rows(hh, "s", zl)

    def add_theirs(hh):
        add_rows(hh, "r", 1 - zl)

    def softmax(hh):
        arrived(("p", hh), pair_in.at[hh])
        totals = [own_rows[hh, half] + pair_in[hh, half].astype(F32) for half in range(2)]
        largest = jnp.max(jnp.maximum(totals[0], totals[1]), axis=-1, keepdims=True)
        weights = [jnp.exp(total - largest) for total in totals]
        scaling = 1.0 / jnp.sum(weights[0] + weights[1], axis=-1, keepdims=True)
        for half in range(2):
            probs[hh, y, :, half * 512:half * 512 + 512] = (weights[half] * scaling).astype(BF16)
        for kind, first in (("a", 0), ("b", 32)):
            for k in (1, 3):
                block = probs.at[hh, y, pl.ds(first if k == 1 else 32 - first, 32)]
                send("a", (kind, hh), block, block, at_y(k))

    def forward_probs(hh):
        for k, first in ((1, 0), (3, 32)):
            arrived(("a", hh), probs.at[hh, 0])
            block = probs.at[hh, lax.rem(y + NY - k, NY), pl.ds(first, 32)]
            send("a", ("b", hh), block, block, at_y(k))

    def attend(stage):
        hh, lo, n = columns(stage)
        arrived(("a", hh), probs.at[hh, 0])
        arrived(("b", hh), probs.at[hh, pl.ds(0, 2)])

        @pl.loop(lo // COLS, (lo + n) // COLS)
        def _(tile):
            at = pl.ds(pl.multiple_of(tile * COLS, COLS), COLS)
            o = jnp.dot(
                probs[hh].reshape(256, 1024), v_all[hh, :, :, :, at].reshape(1024, COLS),
                preferred_element_type=F32,
            )
            att_out[hh, :, :, at] = o.astype(BF16).reshape(NX, 64, COLS)

        at = pl.ds(lo, n)
        att_all[per * x + hh, :, at] = att_out[hh, x, :, at]
        for k in (2, 1, 3):
            to = lax.rem(x + k, NX)
            send("o", ("o", stage), att_out.at[hh, to, :, at], att_all.at[per * x + hh, :, at], at_x(k))

    def swap_weights():
        for load in loads[5:]:
            load.wait()
        for hh in range(per):
            for xp in range(NX):
                wout[1, hh, xp] = wout[0, hh, xp ^ 1]

    def project_out(stage):
        hh, lo, n = columns(stage)
        arrived(("o", stage), att_all.at[pl.ds(0, 3), :, pl.ds(lo, n)])
        m0, m1 = lo // 128, (lo + n) // 128
        for m in range(m0, m1):
            for pair in range(NX // 2):
                a = att_all[2 * pair * per + hh, :, m * 128:m * 128 + 128]
                b = att_all[(2 * pair + 1) * per + hh, :, m * 128:m * 128 + 128]
                lhs[0, m, :, pair * 128:pair * 128 + 128] = a * lows + b * highs
                lhs[1, m, :, pair * 128:pair * 128 + 128] = b * lows + a * highs

        @pl.loop(0, width // COLS)
        def _(tile):
            at = pl.ds(pl.multiple_of(tile * COLS, COLS), COLS)
            for q in range(2):
                s = (hh + q) % 2
                o = jnp.dot(
                    lhs[q, m0:m1].reshape((m1 - m0) * 64, NX * DH), wout[q, hh, :, :, at].reshape(NX * DH, COLS),
                    preferred_element_type=F32,
                ).reshape(m1 - m0, 64, COLS)
                out_ref[m0:m1, s, :, at] = o if hh == 0 else out_ref[m0:m1, s, :, at] + o

    def drain_keys():
        across_z = pl.ds(MORE, width - MORE)
        left("t", tok.at[pl.ds(0, 128)])
        left("kx", k_mine.at[pl.ds(0, 3 * per)])
        left("kt", k_more.at[pl.ds(0, 3 * per)])
        left("kz", k_mine.at[pl.ds(0, 4 * per), :, across_z])
        left("kc", k_all.at[pl.ds(0, per), pl.ds(0, 2)])
        left("q", q_mine.at[pl.ds(0, 3 * per)])
        for kind in ("r", "s"):
            left(kind, part_out.at[pl.ds(0, per), 0, pl.ds(0, 3)])

    def drain_most():
        left("vx", v_mine.at[pl.ds(0, 3 * per)])
        left("vt", v_more.at[pl.ds(0, 3 * per)])
        left("p", pair_out)

    def drain_last():
        left("vz", v_mine.at[pl.ds(0, 4 * per), :, pl.ds(MORE, width - MORE)])
        left("vc", v_all.at[pl.ds(0, per), pl.ds(0, 2)])
        left("a", probs.at[pl.ds(0, per), pl.ds(0, 3)])
        left("o", att_out.at[pl.ds(0, per), pl.ds(0, 3)])

    def start_tokens():
        loads[0].wait()
        pl.semaphore_wait(barrier, len(others))
        send("t", "t", tok.at[pl.ds(0, 128)], tok.at[pl.ds(rows, 128)], at_zl)

    def project_keys():
        loads[1].wait()
        loads[2].wait()
        src, dst, _ = kv["k"]

        def after(n):
            for k in (1, 3, 2):
                to = lax.rem(x + k, NX)
                ready = lax.div(per * to, COLS // DH) == n
                send("kx", ("kx", 0, k), src.at[per * to], dst.at[0, mine, x], at_x(k), ready)

        project(wkv, 0, k_mine, after=after)
        dst[0, mine, x] = src[per * x]

    def project_query():
        loads[3].wait()
        project(wq, 0, q_mine, scale)

    def project_values():
        loads[4].wait()
        project(wkv, half, v_mine)

    start_tokens()
    project_keys()
    kv_own("k", 1)
    kv_send("k", 1)
    kv_more("k")
    kv_forward("k", 0)
    project_query()
    q_send(0)
    q_send(1)
    project_values()
    kv_own("k", 0)
    kv_forward("k", 1)
    kv_own("v", 0)
    kv_send("k", 2)
    kv_own("k", 2)
    q_send(2)
    kv_send("v", 0)
    kv_own("v", 4)
    kv_own("v", 1)
    kv_last("k", 0)
    logits_mine(0)
    logits_theirs(0)
    kv_last("k", 1)
    logits_mine(1)
    kv_send("v", 1)
    kv_forward("k", 2)
    logits_theirs(1)
    kv_more("v")
    kv_send("v", 2)
    add_mine(0)
    add_theirs(0)
    logits_mine(2)
    add_mine(1)
    add_theirs(1)
    kv_last("k", 2)
    logits_theirs(2)
    kv_forward("v", 0)
    softmax(0)
    softmax(1)
    add_mine(2)
    add_theirs(2)
    kv_forward("v", 1)
    kv_own("v", 3)
    forward_probs(0)
    drain_keys()
    kv_last("v", 0)
    forward_probs(1)
    softmax(2)
    kv_forward("v", 3)
    attend(0)
    swap_weights()
    kv_forward("v", 4)
    kv_last("v", 1)
    attend(1)
    forward_probs(2)
    drain_most()
    kv_last("v", 3)
    attend(3)
    kv_last("v", 4)
    attend(4)
    project_out(0)
    project_out(1)
    project_out(3)
    project_out(4)

    drain_last()


def local(tokens, w_query, w_keyval, w_out):
    seq_dev, res_dev, width = tokens.shape
    heads = width // DH
    per = heads // NX
    scale = 1.0 / math.sqrt(DH * seq_dev * lax.axis_size("seq"))
    rows = seq_dev * res_dev
    block = (heads, res_dev, seq_dev * DH)
    mixed = pl.pallas_call(
        functools.partial(layer_kernel, scale),
        out_shape=jax.ShapeDtypeStruct((seq_dev // 2, 2, res_dev, width), F32),
        in_specs=[pl.BlockSpec(memory_space=pltpu.HBM)] * 4,
        out_specs=pl.BlockSpec(memory_space=pltpu.VMEM),
        scratch_shapes=[
            pltpu.VMEM((rows + 128, width), BF16),
            pltpu.VMEM((width, width), BF16),
            pltpu.VMEM((width, 2 * width), BF16),
            pltpu.VMEM((2, per, NX, DH, width), BF16),
            pltpu.VMEM(block, BF16),
            pltpu.VMEM(block, BF16),
            pltpu.VMEM(block, BF16),
            pltpu.VMEM((heads, res_dev, MORE), BF16),
            pltpu.VMEM((heads, res_dev, MORE), BF16),
            pltpu.VMEM((per, NX, res_dev, seq_dev * DH), BF16),
            pltpu.VMEM((per, 4, NX, res_dev, seq_dev * DH), BF16),
            pltpu.VMEM((per, 4, NX, res_dev, seq_dev * DH), BF16),
            pltpu.VMEM((NX, res_dev, 512), F32),
            pltpu.VMEM((per, 2, NY, res_dev, 512), BF16),
            pltpu.VMEM((per, 2, 3, res_dev, 512), BF16),
            pltpu.VMEM((per, 2, res_dev, 512), F32),
            pltpu.VMEM((per, 2, res_dev, 512), BF16),
            pltpu.VMEM((per, 2, res_dev, 512), BF16),
            pltpu.VMEM((per, NY, res_dev, 1024), BF16),
            pltpu.VMEM((per, NX, res_dev, seq_dev * DH), BF16),
            pltpu.VMEM(block, BF16),
            pltpu.VMEM((2, seq_dev // 2, res_dev, NX * DH), BF16),
            pltpu.SemaphoreType.DMA((8,)),
            pltpu.SemaphoreType.DMA((15,)),
            pltpu.SemaphoreType.DMA((54,)),
        ],
        cost_estimate=pl.CostEstimate(flops=6 * 10**9, bytes_accessed=10**7, transcendentals=2 * 10**5),
        compiler_params=pltpu.CompilerParams(
            collective_id=0, has_side_effects=True, vmem_limit_bytes=44 * 2**20
        ),
        name="tied_row_attention",
    )(*[pltpu.with_memory_space_constraint(a, pltpu.HBM) for a in (tokens.reshape(rows, width), w_query, w_keyval, w_out.reshape(NX, per, DH, width))])
    return mixed.reshape(seq_dev, res_dev, width)


def solution(mesh):
    return jax.shard_map(
        local,
        mesh=mesh,
        in_specs=(P("seq", "res", None), P(), P(), P()),
        out_specs=P("seq", "res", None),
        check_vma=False,
    )
```

```python
import functools
import math

import jax
import jax.numpy as jnp
from jax import lax
from jax.experimental import pallas as pl
from jax.experimental.pallas import tpu as pltpu
from jax.sharding import PartitionSpec as P

DH = 64
NX, NY = 4, 4
COLS = 256
MORE = 128
MESH = pl.DeviceIdType.MESH
BF16, F32 = jnp.bfloat16, jnp.float32


def layer_kernel(
    scale,
    tok_hbm, wq_hbm, wkv_hbm, wout_ref, out_ref,
    tok, wq, wkv, wout, q_mine, k_mine, v_mine, k_more, v_more, q_all, k_all, v_all,
    scores, part_out, part_in, own_rows, pair_out, pair_in, probs, att_out, att_all, lhs,
    load_sem, send_sem, recv_sem,
):
    seq, res = lax.axis_index("seq"), lax.axis_index("res")
    y, zh = lax.div(seq, 2), lax.rem(seq, 2)
    zl, x, c = lax.div(res, 8), lax.rem(lax.div(res, 2), NX), lax.rem(res, 2)
    rows, width = tok_hbm.shape
    heads = q_mine.shape[0]
    per = heads // NX

    def at_x(k):
        return (seq, zl * 8 + lax.rem(x + k, NX) * 2 + c)

    def at_y(k):
        return (lax.rem(y + k, NY) * 2 + zh, res)

    at_zl = (seq, (1 - zl) * 8 + x * 2 + c)
    at_core = (seq, zl * 8 + x * 2 + (1 - c))
    at_zh = (y * 2 + (1 - zh), res)

    senders, receivers, seen = {}, {}, set()

    def send(kind, group, src, dst, where, when=None):
        copy = pltpu.make_async_remote_copy(
            src_ref=src, dst_ref=dst,
            send_sem=send_sem.at[senders.setdefault(kind, len(senders))],
            recv_sem=recv_sem.at[receivers.setdefault(group, len(receivers))],
            device_id=where, device_id_type=MESH,
        )
        if when is None:
            copy.start()
        else:
            pl.when(when)(copy.start)

    def arrived(group, ref):
        if group not in seen:
            seen.add(group)
            pltpu.make_async_copy(ref, ref, recv_sem.at[receivers[group]]).wait()

    def left(kind, ref):
        pltpu.make_async_copy(ref, ref, send_sem.at[senders[kind]]).wait()

    half = wkv.shape[1] // 2
    loads = [
        pltpu.make_async_copy(tok_hbm.at[pl.ds(0, 128)], tok.at[pl.ds(0, 128)], load_sem.at[0]),
        pltpu.make_async_copy(tok_hbm.at[pl.ds(128, rows - 128)], tok.at[pl.ds(128, rows - 128)], load_sem.at[1]),
        pltpu.make_async_copy(wkv_hbm.at[:, pl.ds(0, half)], wkv.at[:, pl.ds(0, half)], load_sem.at[2]),
        pltpu.make_async_copy(wq_hbm, wq, load_sem.at[3]),
        pltpu.make_async_copy(wkv_hbm.at[:, pl.ds(half, half)], wkv.at[:, pl.ds(half, half)], load_sem.at[4]),
    ] + [pltpu.make_async_copy(wout_ref.at[:, hh], wout.at[0, hh], load_sem.at[5 + hh]) for hh in range(per)]
    for load in loads[:3]:
        load.start()

    barrier = pltpu.get_barrier_semaphore()
    others = [at_x(1), at_x(2), at_x(3), at_y(1), at_y(2), at_y(3), at_zl, at_core, at_zh]
    for other in others:
        pl.semaphore_signal(barrier, inc=1, device_id=other, device_id_type=MESH)
    for load in loads[3:]:
        load.start()

    low = lax.broadcasted_iota(jnp.int32, (64, 128), 1) < DH
    lows = jnp.where(low, 1.0, 0.0).astype(BF16)
    highs = jnp.where(low, 0.0, 1.0).astype(BF16)

    def project(w, first, dst, factor=None, row=0, pairs=rows // 128, after=None):
        def tile(n):
            at = first + n * COLS if after else pl.multiple_of(first + n * COLS, COLS)
            acc = jnp.dot(tok[row:row + pairs * 128], w[:, pl.ds(at, COLS)], preferred_element_type=F32)
            if factor is not None:
                acc = acc * factor
            for pair in range(COLS // 128):
                for m in range(pairs):
                    even = acc[m * 128:m * 128 + 64, pair * 128:pair * 128 + 128]
                    odd = pltpu.roll(acc[m * 128 + 64:m * 128 + 128, pair * 128:pair * 128 + 128], 64, 1)
                    head = n * (COLS // DH) + 2 * pair
                    dst[head, :, m * 128:m * 128 + 128] = jnp.where(low, even, odd).astype(BF16)
                    dst[head + 1, :, m * 128:m * 128 + 128] = jnp.where(low, odd, even).astype(BF16)

        if after is None:
            pl.loop(0, width // COLS)(tile)
        else:
            for n in range(width // COLS):
                tile(n)
                after(n)

    mine = zl * 2 + c
    theirs = (1 - zl) * 2 + c
    kv = {"k": (k_mine, k_all, k_more), "v": (v_mine, v_all, v_more)}

    def columns(stage):
        return {2: (2, 0, width), 3: (2, 0, 512), 4: (2, 512, 256)}.get(stage, (stage, 0, width))

    def kv_send(kind, hh):
        src, dst, _ = kv[kind]
        dst[hh, mine, x] = src[per * x + hh]
        for k in (1, 3, 2):
            to = lax.rem(x + k, NX)
            group = (kind + "x", hh, k if kind == "k" else 0)
            send(kind + "x", group, src.at[per * to + hh], dst.at[hh, mine, x], at_x(k))

    def kv_more(kind):
        arrived("t", tok.at[pl.ds(rows, 128)])
        _, dst, src = kv[kind]
        project(wkv, 0 if kind == "k" else half, src, row=rows, pairs=1)
        for hh in range(per):
            dst[hh, theirs, x, :, 0:MORE] = src[per * x + hh]
        for k in (2, 1, 3):
            to = lax.rem(x + k, NX)
            send(
                kind + "t", kind + "t", src.at[pl.ds(per * to, per)],
                dst.at[pl.ds(0, per), theirs, x, :, pl.ds(0, MORE)], at_x(k),
            )

    def across(stage):
        hh, lo, n = columns(stage)
        first = max(lo, MORE)
        return hh, pl.ds(first, lo + n - first)

    def kv_own(kind, stage):
        src, dst, _ = kv[kind]
        hh, at = across(stage)
        send(kind + "z", (kind + "z", stage), src.at[per * x + hh, :, at], dst.at[hh, mine, x, :, at], at_zl)

    def kv_forward(kind, stage):
        _, dst, _ = kv[kind]
        hh, at = across(stage)
        for k in (1, 3, 2):
            block = dst.at[hh, mine, lax.rem(x + NX - k, NX)]
            if kind == "k":
                arrived(("kx", hh, k), block)
            else:
                arrived(("vx", hh, 0), dst.at[hh, mine, pl.ds(0, 3)])
            block = block.at[:, at]
            send(kind + "z", (kind + "z", stage), block, block, at_zl)
        hh, lo, n = columns(stage)
        blocks = dst.at[hh, mine, :, :, pl.ds(lo, n)]
        send(kind + "c", (kind + "c", stage, 0), blocks, blocks, at_core)

    def kv_last(kind, stage):
        _, dst, _ = kv[kind]
        arrived(kind + "t", dst.at[pl.ds(0, per), theirs, pl.ds(0, 3), :, pl.ds(0, MORE)])
        hh, at = across(stage)
        arrived((kind + "z", stage), dst.at[hh, theirs, :, :, at])
        hh, lo, n = columns(stage)
        at = pl.ds(lo, n)
        blocks = dst.at[hh, theirs, :, :, at]
        if kind == "k":
            send("kc", ("kc", stage, 1), blocks, blocks, at_core)
            arrived(("kc", stage, 0), dst.at[hh, 2 * zl + 1 - c])
            arrived(("kc", stage, 1), dst.at[hh, 2 * (1 - zl) + 1 - c])
        else:
            send("vc", ("vc", stage, 0), blocks, blocks, at_core)
            arrived(("vc", stage, 0), dst.at[hh, pl.ds(0, 2), :, :, at])

    def q_send(hh):
        q_all[hh, x] = q_mine[per * x + hh]
        for k in (2, 1, 3):
            to = lax.rem(x + k, NX)
            send("q", ("q", hh), q_mine.at[per * to + hh], q_all.at[hh, x], at_x(k))

    def logits(hh, half):
        arrived(("q", hh), q_all.at[hh, pl.ds(0, 3)])

        @pl.loop(0, 2)
        def _(t):
            s = lax.dot_general(
                q_all[hh].reshape(256, width), k_all[hh, half * 2 + t].reshape(256, width),
                (((1,), (1,)), ((), ())), preferred_element_type=F32,
            ).reshape(NX, 64, 256)
            at = pl.ds(pl.multiple_of(t * 256, 256), 256)
            scores[:, :, at] = s
            part_out[hh, half, :, :, at] = s.astype(BF16)

        own_rows[hh, half] = scores[y]

    def send_rows(kind, hh, half):
        for k in (2, 1, 3):
            send(
                kind, (kind, hh), part_out.at[hh, half, lax.rem(y + k, NY)], part_in.at[hh, half, k - 1], at_y(k)
            )

    def logits_mine(hh):
        arrived(("kc", hh, 0), k_all.at[hh, 2 * zl + 1 - c])
        logits(hh, zl)
        send_rows("s", hh, zl)

    def logits_theirs(hh):
        logits(hh, 1 - zl)
        send_rows("r", hh, 1 - zl)

    def add_rows(hh, kind, half):
        arrived((kind, hh), part_in.at[hh, half])
        total = own_rows[hh, half]
        for k in range(3):
            total = total + part_in[hh, half, k].astype(F32)
        own_rows[hh, half] = total
        pair_out[hh, half] = total.astype(BF16)
        send("p", ("p", hh), pair_out.at[hh, half], pair_in.at[hh, half], at_zh)

    def add_mine(hh):
        add_rows(hh, "s", zl)

    def add_theirs(hh):
        add_rows(hh, "r", 1 - zl)

    def softmax(hh):
        arrived(("p", hh), pair_in.at[hh])
        totals = [own_rows[hh, half] + pair_in[hh, half].astype(F32) for half in range(2)]
        largest = jnp.max(jnp.maximum(totals[0], totals[1]), axis=-1, keepdims=True)
        weights = [jnp.exp(total - largest) for total in totals]
        scaling = 1.0 / jnp.sum(weights[0] + weights[1], axis=-1, keepdims=True)
        for half in range(2):
            probs[hh, y, :, half * 512:half * 512 + 512] = (weights[half] * scaling).astype(BF16)
        for kind, first in (("a", 0), ("b", 32)):
            for k in (1, 3):
                block = probs.at[hh, y, pl.ds(first if k == 1 else 32 - first, 32)]
                send("a", (kind, hh), block, block, at_y(k))

    def forward_probs(hh):
        for k, first in ((1, 0), (3, 32)):
            arrived(("a", hh), probs.at[hh, 0])
            block = probs.at[hh, lax.rem(y + NY - k, NY), pl.ds(first, 32)]
            send("a", ("b", hh), block, block, at_y(k))

    def attend(stage):
        hh, lo, n = columns(stage)
        arrived(("a", hh), probs.at[hh, 0])
        arrived(("b", hh), probs.at[hh, pl.ds(0, 2)])

        @pl.loop(lo // COLS, (lo + n) // COLS)
        def _(tile):
            at = pl.ds(pl.multiple_of(tile * COLS, COLS), COLS)
            o = jnp.dot(
                probs[hh].reshape(256, 1024), v_all[hh, :, :, :, at].reshape(1024, COLS),
                preferred_element_type=F32,
            )
            att_out[hh, :, :, at] = o.astype(BF16).reshape(NX, 64, COLS)

        at = pl.ds(lo, n)
        att_all[per * x + hh, :, at] = att_out[hh, x, :, at]
        for k in (2, 1, 3):
            to = lax.rem(x + k, NX)
            send("o", ("o", stage), att_out.at[hh, to, :, at], att_all.at[per * x + hh, :, at], at_x(k))

    def swap_weights():
        for load in loads[5:]:
            load.wait()
        for hh in range(per):
            for xp in range(NX):
                wout[1, hh, xp] = wout[0, hh, xp ^ 1]

    def project_out(stage):
        hh, lo, n = columns(stage)
        arrived(("o", stage), att_all.at[pl.ds(0, 3), :, pl.ds(lo, n)])
        m0, m1 = lo // 128, (lo + n) // 128
        for m in range(m0, m1):
            for pair in range(NX // 2):
                a = att_all[2 * pair * per + hh, :, m * 128:m * 128 + 128]
                b = att_all[(2 * pair + 1) * per + hh, :, m * 128:m * 128 + 128]
                lhs[0, m, :, pair * 128:pair * 128 + 128] = a * lows + b * highs
                lhs[1, m, :, pair * 128:pair * 128 + 128] = b * lows + a * highs

        @pl.loop(0, width // COLS)
        def _(tile):
            at = pl.ds(pl.multiple_of(tile * COLS, COLS), COLS)
            for q in range(2):
                s = (hh + q) % 2
                o = jnp.dot(
                    lhs[q, m0:m1].reshape((m1 - m0) * 64, NX * DH), wout[q, hh, :, :, at].reshape(NX * DH, COLS),
                    preferred_element_type=F32,
                ).reshape(m1 - m0, 64, COLS)
                out_ref[m0:m1, s, :, at] = o if hh == 0 else out_ref[m0:m1, s, :, at] + o

    def drain_keys():
        across_z = pl.ds(MORE, width - MORE)
        left("t", tok.at[pl.ds(0, 128)])
        left("kx", k_mine.at[pl.ds(0, 3 * per)])
        left("kt", k_more.at[pl.ds(0, 3 * per)])
        left("kz", k_mine.at[pl.ds(0, 4 * per), :, across_z])
        left("kc", k_all.at[pl.ds(0, per), pl.ds(0, 2)])
        left("q", q_mine.at[pl.ds(0, 3 * per)])
        for kind in ("r", "s"):
            left(kind, part_out.at[pl.ds(0, per), 0, pl.ds(0, 3)])

    def drain_most():
        left("vx", v_mine.at[pl.ds(0, 3 * per)])
        left("vt", v_more.at[pl.ds(0, 3 * per)])
        left("p", pair_out)

    def drain_last():
        left("vz", v_mine.at[pl.ds(0, 4 * per), :, pl.ds(MORE, width - MORE)])
        left("vc", v_all.at[pl.ds(0, per), pl.ds(0, 2)])
        left("a", probs.at[pl.ds(0, per), pl.ds(0, 3)])
        left("o", att_out.at[pl.ds(0, per), pl.ds(0, 3)])

    def start_tokens():
        loads[0].wait()
        pl.semaphore_wait(barrier, len(others))
        send("t", "t", tok.at[pl.ds(0, 128)], tok.at[pl.ds(rows, 128)], at_zl)

    def project_keys():
        loads[1].wait()
        loads[2].wait()
        src, dst, _ = kv["k"]

        def after(n):
            for k in (1, 3, 2):
                to = lax.rem(x + k, NX)
                ready = lax.div(per * to, COLS // DH) == n
                send("kx", ("kx", 0, k), src.at[per * to], dst.at[0, mine, x], at_x(k), ready)

        project(wkv, 0, k_mine, after=after)
        dst[0, mine, x] = src[per * x]

    def project_query():
        loads[3].wait()
        project(wq, 0, q_mine, scale)

    def project_values():
        loads[4].wait()
        project(wkv, half, v_mine)

    start_tokens()
    project_keys()
    kv_own("k", 0)
    project_query()
    q_send(0)
    project_values()
    kv_own("k", 2)
    kv_send("k", 1)
    kv_own("k", 1)
    kv_more("k")
    q_send(1)
    kv_forward("k", 0)
    kv_send("k", 2)
    kv_forward("k", 1)
    logits_mine(0)
    kv_own("v", 1)
    q_send(2)
    kv_last("k", 0)
    kv_own("v", 0)
    logits_theirs(0)
    add_mine(0)
    kv_send("v", 0)
    logits_mine(1)
    kv_last("k", 1)
    kv_forward("k", 2)
    add_theirs(0)
    logits_theirs(1)
    kv_send("v", 1)
    kv_more("v")
    logits_mine(2)
    add_mine(1)
    swap_weights()
    add_theirs(1)
    kv_last("k", 2)
    kv_forward("v", 0)
    logits_theirs(2)
    drain_keys()
    softmax(0)
    kv_send("v", 2)
    add_mine(2)
    add_theirs(2)
    softmax(1)
    kv_forward("v", 1)
    forward_probs(0)
    kv_last("v", 0)
    forward_probs(1)
    kv_forward("v", 3)
    kv_own("v", 3)
    kv_own("v", 4)
    kv_forward("v", 4)
    softmax(2)
    attend(0)
    kv_last("v", 1)
    forward_probs(2)
    attend(1)
    drain_most()
    kv_last("v", 3)
    attend(3)
    kv_last("v", 4)
    attend(4)
    project_out(0)
    project_out(1)
    project_out(3)
    project_out(4)

    drain_last()


def local(tokens, w_query, w_keyval, w_out):
    seq_dev, res_dev, width = tokens.shape
    heads = width // DH
    per = heads // NX
    scale = 1.0 / math.sqrt(DH * seq_dev * lax.axis_size("seq"))
    rows = seq_dev * res_dev
    block = (heads, res_dev, seq_dev * DH)
    mixed = pl.pallas_call(
        functools.partial(layer_kernel, scale),
        out_shape=jax.ShapeDtypeStruct((seq_dev // 2, 2, res_dev, width), F32),
        in_specs=[pl.BlockSpec(memory_space=pltpu.HBM)] * 4,
        out_specs=pl.BlockSpec(memory_space=pltpu.VMEM),
        scratch_shapes=[
            pltpu.VMEM((rows + 128, width), BF16),
            pltpu.VMEM((width, width), BF16),
            pltpu.VMEM((width, 2 * width), BF16),
            pltpu.VMEM((2, per, NX, DH, width), BF16),
            pltpu.VMEM(block, BF16),
            pltpu.VMEM(block, BF16),
            pltpu.VMEM(block, BF16),
            pltpu.VMEM((heads, res_dev, MORE), BF16),
            pltpu.VMEM((heads, res_dev, MORE), BF16),
            pltpu.VMEM((per, NX, res_dev, seq_dev * DH), BF16),
            pltpu.VMEM((per, 4, NX, res_dev, seq_dev * DH), BF16),
            pltpu.VMEM((per, 4, NX, res_dev, seq_dev * DH), BF16),
            pltpu.VMEM((NX, res_dev, 512), F32),
            pltpu.VMEM((per, 2, NY, res_dev, 512), BF16),
            pltpu.VMEM((per, 2, 3, res_dev, 512), BF16),
            pltpu.VMEM((per, 2, res_dev, 512), F32),
            pltpu.VMEM((per, 2, res_dev, 512), BF16),
            pltpu.VMEM((per, 2, res_dev, 512), BF16),
            pltpu.VMEM((per, NY, res_dev, 1024), BF16),
            pltpu.VMEM((per, NX, res_dev, seq_dev * DH), BF16),
            pltpu.VMEM(block, BF16),
            pltpu.VMEM((2, seq_dev // 2, res_dev, NX * DH), BF16),
            pltpu.SemaphoreType.DMA((8,)),
            pltpu.SemaphoreType.DMA((15,)),
            pltpu.SemaphoreType.DMA((54,)),
        ],
        cost_estimate=pl.CostEstimate(flops=6 * 10**9, bytes_accessed=10**7, transcendentals=2 * 10**5),
        compiler_params=pltpu.CompilerParams(
            collective_id=0, has_side_effects=True, vmem_limit_bytes=44 * 2**20
        ),
        name="tied_row_attention",
    )(*[pltpu.with_memory_space_constraint(a, pltpu.HBM) for a in (tokens.reshape(rows, width), w_query, w_keyval, w_out.reshape(NX, per, DH, width))])
    return mixed.reshape(seq_dev, res_dev, width)


def solution(mesh):
    return jax.shard_map(
        local,
        mesh=mesh,
        in_specs=(P("seq", "res", None), P(), P(), P()),
        out_specs=P("seq", "res", None),
        check_vma=False,
    )
```

```python
import functools
import math

import jax
import jax.numpy as jnp
from jax import lax
from jax.experimental import pallas as pl
from jax.experimental.pallas import tpu as pltpu
from jax.sharding import PartitionSpec as P

DH = 64
NX, NY = 4, 4
COLS = 256
MORE = 128
MESH = pl.DeviceIdType.MESH
BF16, F32 = jnp.bfloat16, jnp.float32


def layer_kernel(
    scale,
    tok_hbm, wq_hbm, wkv_hbm, wout_ref, out_ref,
    tok, wq, wkv, wout, q_mine, k_mine, v_mine, k_more, v_more, q_all, k_all, v_all,
    scores, part_out, part_in, own_rows, pair_out, pair_in, probs, att_out, att_all, lhs,
    load_sem, send_sem, recv_sem,
):
    seq, res = lax.axis_index("seq"), lax.axis_index("res")
    y, zh = lax.div(seq, 2), lax.rem(seq, 2)
    zl, x, c = lax.div(res, 8), lax.rem(lax.div(res, 2), NX), lax.rem(res, 2)
    rows, width = tok_hbm.shape
    heads = q_mine.shape[0]
    per = heads // NX

    def at_x(k):
        return (seq, zl * 8 + lax.rem(x + k, NX) * 2 + c)

    def at_y(k):
        return (lax.rem(y + k, NY) * 2 + zh, res)

    at_zl = (seq, (1 - zl) * 8 + x * 2 + c)
    at_core = (seq, zl * 8 + x * 2 + (1 - c))
    at_zh = (y * 2 + (1 - zh), res)

    senders, receivers, seen = {}, {}, set()

    def send(kind, group, src, dst, where, when=None):
        copy = pltpu.make_async_remote_copy(
            src_ref=src, dst_ref=dst,
            send_sem=send_sem.at[senders.setdefault(kind, len(senders))],
            recv_sem=recv_sem.at[receivers.setdefault(group, len(receivers))],
            device_id=where, device_id_type=MESH,
        )
        if when is None:
            copy.start()
        else:
            pl.when(when)(copy.start)

    def arrived(group, ref):
        if group not in seen:
            seen.add(group)
            pltpu.make_async_copy(ref, ref, recv_sem.at[receivers[group]]).wait()

    def left(kind, ref):
        pltpu.make_async_copy(ref, ref, send_sem.at[senders[kind]]).wait()

    half = wkv.shape[1] // 2
    loads = [
        pltpu.make_async_copy(tok_hbm.at[pl.ds(0, 128)], tok.at[pl.ds(0, 128)], load_sem.at[0]),
        pltpu.make_async_copy(wkv_hbm.at[:, pl.ds(0, half)], wkv.at[:, pl.ds(0, half)], load_sem.at[1]),
        pltpu.make_async_copy(tok_hbm.at[pl.ds(128, rows - 128)], tok.at[pl.ds(128, rows - 128)], load_sem.at[2]),
        pltpu.make_async_copy(wq_hbm, wq, load_sem.at[3]),
        pltpu.make_async_copy(wkv_hbm.at[:, pl.ds(half, half)], wkv.at[:, pl.ds(half, half)], load_sem.at[4]),
    ] + [pltpu.make_async_copy(wout_ref.at[:, hh], wout.at[0, hh], load_sem.at[5 + hh]) for hh in range(per)]
    for load in loads[:3]:
        load.start()

    barrier = pltpu.get_barrier_semaphore()
    others = [at_x(1), at_x(2), at_x(3), at_y(1), at_y(2), at_y(3), at_zl, at_core, at_zh]
    for other in others:
        pl.semaphore_signal(barrier, inc=1, device_id=other, device_id_type=MESH)
    for load in loads[3:]:
        load.start()

    low = lax.broadcasted_iota(jnp.int32, (64, 128), 1) < DH
    lows = jnp.where(low, 1.0, 0.0).astype(BF16)
    highs = jnp.where(low, 0.0, 1.0).astype(BF16)

    def project(w, first, dst, factor=None, row=0, pairs=rows // 128, after=None):
        def tile(n):
            at = first + n * COLS if after else pl.multiple_of(first + n * COLS, COLS)
            acc = jnp.dot(tok[row:row + pairs * 128], w[:, pl.ds(at, COLS)], preferred_element_type=F32)
            if factor is not None:
                acc = acc * factor
            for pair in range(COLS // 128):
                for m in range(pairs):
                    even = acc[m * 128:m * 128 + 64, pair * 128:pair * 128 + 128]
                    odd = pltpu.roll(acc[m * 128 + 64:m * 128 + 128, pair * 128:pair * 128 + 128], 64, 1)
                    head = n * (COLS // DH) + 2 * pair
                    dst[head, :, m * 128:m * 128 + 128] = jnp.where(low, even, odd).astype(BF16)
                    dst[head + 1, :, m * 128:m * 128 + 128] = jnp.where(low, odd, even).astype(BF16)

        if after is None:
            pl.loop(0, width // COLS)(tile)
        else:
            for n in range(width // COLS):
                tile(n)
                after(n)

    mine = zl * 2 + c
    theirs = (1 - zl) * 2 + c
    kv = {"k": (k_mine, k_all, k_more), "v": (v_mine, v_all, v_more)}

    def columns(stage):
        return {2: (2, 0, width), 3: (2, 0, 512), 4: (2, 512, 256)}.get(stage, (stage, 0, width))

    def kv_send(kind, hh):
        src, dst, _ = kv[kind]
        dst[hh, mine, x] = src[per * x + hh]
        for k in (1, 3, 2):
            to = lax.rem(x + k, NX)
            group = (kind + "x", hh, k if kind == "k" else 0)
            send(kind + "x", group, src.at[per * to + hh], dst.at[hh, mine, x], at_x(k))

    def kv_more(kind):
        arrived("t", tok.at[pl.ds(rows, 128)])
        _, dst, src = kv[kind]
        project(wkv, 0 if kind == "k" else half, src, row=rows, pairs=1)
        for hh in range(per):
            dst[hh, theirs, x, :, 0:MORE] = src[per * x + hh]
        for k in (2, 1, 3):
            to = lax.rem(x + k, NX)
            send(
                kind + "t", kind + "t", src.at[pl.ds(per * to, per)],
                dst.at[pl.ds(0, per), theirs, x, :, pl.ds(0, MORE)], at_x(k),
            )

    def across(stage):
        hh, lo, n = columns(stage)
        first = max(lo, MORE)
        return hh, pl.ds(first, lo + n - first)

    def kv_own(kind, stage):
        src, dst, _ = kv[kind]
        hh, at = across(stage)
        send(kind + "z", (kind + "z", stage), src.at[per * x + hh, :, at], dst.at[hh, mine, x, :, at], at_zl)

    def kv_forward(kind, stage):
        _, dst, _ = kv[kind]
        hh, at = across(stage)
        for k in (1, 3, 2):
            block = dst.at[hh, mine, lax.rem(x + NX - k, NX)]
            if kind == "k":
                arrived(("kx", hh, k), block)
            else:
                arrived(("vx", hh, 0), dst.at[hh, mine, pl.ds(0, 3)])
            block = block.at[:, at]
            send(kind + "z", (kind + "z", stage), block, block, at_zl)
        hh, lo, n = columns(stage)
        blocks = dst.at[hh, mine, :, :, pl.ds(lo, n)]
        send(kind + "c", (kind + "c", stage, 0), blocks, blocks, at_core)

    def kv_last(kind, stage):
        _, dst, _ = kv[kind]
        arrived(kind + "t", dst.at[pl.ds(0, per), theirs, pl.ds(0, 3), :, pl.ds(0, MORE)])
        hh, at = across(stage)
        arrived((kind + "z", stage), dst.at[hh, theirs, :, :, at])
        hh, lo, n = columns(stage)
        at = pl.ds(lo, n)
        blocks = dst.at[hh, theirs, :, :, at]
        if kind == "k":
            send("kc", ("kc", stage, 1), blocks, blocks, at_core)
            arrived(("kc", stage, 0), dst.at[hh, 2 * zl + 1 - c])
            arrived(("kc", stage, 1), dst.at[hh, 2 * (1 - zl) + 1 - c])
        else:
            send("vc", ("vc", stage, 0), blocks, blocks, at_core)
            arrived(("vc", stage, 0), dst.at[hh, pl.ds(0, 2), :, :, at])

    def q_send(hh):
        q_all[hh, x] = q_mine[per * x + hh]
        for k in (2, 1, 3):
            to = lax.rem(x + k, NX)
            send("q", ("q", hh), q_mine.at[per * to + hh], q_all.at[hh, x], at_x(k))

    def logits(hh, half):
        arrived(("q", hh), q_all.at[hh, pl.ds(0, 3)])

        @pl.loop(0, 2)
        def _(t):
            s = lax.dot_general(
                q_all[hh].reshape(256, width), k_all[hh, half * 2 + t].reshape(256, width),
                (((1,), (1,)), ((), ())), preferred_element_type=F32,
            ).reshape(NX, 64, 256)
            at = pl.ds(pl.multiple_of(t * 256, 256), 256)
            scores[:, :, at] = s
            part_out[hh, half, :, :, at] = s.astype(BF16)

        own_rows[hh, half] = scores[y]

    def send_rows(kind, hh, half):
        for k in (2, 1, 3):
            send(
                kind, (kind, hh), part_out.at[hh, half, lax.rem(y + k, NY)], part_in.at[hh, half, k - 1], at_y(k)
            )

    def logits_mine(hh):
        arrived(("kc", hh, 0), k_all.at[hh, 2 * zl + 1 - c])
        logits(hh, zl)
        send_rows("s", hh, zl)

    def logits_theirs(hh):
        logits(hh, 1 - zl)
        send_rows("r", hh, 1 - zl)

    def add_rows(hh, kind, half):
        arrived((kind, hh), part_in.at[hh, half])
        total = own_rows[hh, half]
        for k in range(3):
            total = total + part_in[hh, half, k].astype(F32)
        own_rows[hh, half] = total
        pair_out[hh, half] = total.astype(BF16)
        send("p", ("p", hh), pair_out.at[hh, half], pair_in.at[hh, half], at_zh)

    def add_mine(hh):
        add_rows(hh, "s", zl)

    def add_theirs(hh):
        add_rows(hh, "r", 1 - zl)

    def softmax(hh):
        arrived(("p", hh), pair_in.at[hh])
        totals = [own_rows[hh, half] + pair_in[hh, half].astype(F32) for half in range(2)]
        largest = jnp.max(jnp.maximum(totals[0], totals[1]), axis=-1, keepdims=True)
        weights = [jnp.exp(total - largest) for total in totals]
        scaling = 1.0 / jnp.sum(weights[0] + weights[1], axis=-1, keepdims=True)
        for half in range(2):
            probs[hh, y, :, half * 512:half * 512 + 512] = (weights[half] * scaling).astype(BF16)
        for kind, first in (("a", 0), ("b", 32)):
            for k in (1, 3):
                block = probs.at[hh, y, pl.ds(first if k == 1 else 32 - first, 32)]
                send("a", (kind, hh), block, block, at_y(k))

    def forward_probs(hh):
        for k, first in ((1, 0), (3, 32)):
            arrived(("a", hh), probs.at[hh, 0])
            block = probs.at[hh, lax.rem(y + NY - k, NY), pl.ds(first, 32)]
            send("a", ("b", hh), block, block, at_y(k))

    def attend(stage):
        hh, lo, n = columns(stage)
        arrived(("a", hh), probs.at[hh, 0])
        arrived(("b", hh), probs.at[hh, pl.ds(0, 2)])

        @pl.loop(lo // COLS, (lo + n) // COLS)
        def _(tile):
            at = pl.ds(pl.multiple_of(tile * COLS, COLS), COLS)
            o = jnp.dot(
                probs[hh].reshape(256, 1024), v_all[hh, :, :, :, at].reshape(1024, COLS),
                preferred_element_type=F32,
            )
            att_out[hh, :, :, at] = o.astype(BF16).reshape(NX, 64, COLS)

        at = pl.ds(lo, n)
        att_all[per * x + hh, :, at] = att_out[hh, x, :, at]
        for k in (2, 1, 3):
            to = lax.rem(x + k, NX)
            send("o", ("o", stage), att_out.at[hh, to, :, at], att_all.at[per * x + hh, :, at], at_x(k))

    def swap_weights():
        for load in loads[5:]:
            load.wait()
        for hh in range(per):
            for xp in range(NX):
                wout[1, hh, xp] = wout[0, hh, xp ^ 1]

    def project_out(stage):
        hh, lo, n = columns(stage)
        arrived(("o", stage), att_all.at[pl.ds(0, 3), :, pl.ds(lo, n)])
        m0, m1 = lo // 128, (lo + n) // 128
        for m in range(m0, m1):
            for pair in range(NX // 2):
                a = att_all[2 * pair * per + hh, :, m * 128:m * 128 + 128]
                b = att_all[(2 * pair + 1) * per + hh, :, m * 128:m * 128 + 128]
                lhs[0, m, :, pair * 128:pair * 128 + 128] = a * lows + b * highs
                lhs[1, m, :, pair * 128:pair * 128 + 128] = b * lows + a * highs

        @pl.loop(0, width // COLS)
        def _(tile):
            at = pl.ds(pl.multiple_of(tile * COLS, COLS), COLS)
            for q in range(2):
                s = (hh + q) % 2
                o = jnp.dot(
                    lhs[q, m0:m1].reshape((m1 - m0) * 64, NX * DH), wout[q, hh, :, :, at].reshape(NX * DH, COLS),
                    preferred_element_type=F32,
                ).reshape(m1 - m0, 64, COLS)
                out_ref[m0:m1, s, :, at] = o if hh == 0 else out_ref[m0:m1, s, :, at] + o

    def drain_keys():
        across_z = pl.ds(MORE, width - MORE)
        left("t", tok.at[pl.ds(0, 128)])
        left("kx", k_mine.at[pl.ds(0, 3 * per)])
        left("kt", k_more.at[pl.ds(0, 3 * per)])
        left("kz", k_mine.at[pl.ds(0, 4 * per), :, across_z])
        left("kc", k_all.at[pl.ds(0, per), pl.ds(0, 2)])
        left("q", q_mine.at[pl.ds(0, 3 * per)])
        for kind in ("r", "s"):
            left(kind, part_out.at[pl.ds(0, per), 0, pl.ds(0, 3)])

    def drain_most():
        left("vx", v_mine.at[pl.ds(0, 3 * per)])
        left("vt", v_more.at[pl.ds(0, 3 * per)])
        left("p", pair_out)

    def drain_last():
        left("vz", v_mine.at[pl.ds(0, 4 * per), :, pl.ds(MORE, width - MORE)])
        left("vc", v_all.at[pl.ds(0, per), pl.ds(0, 2)])
        left("a", probs.at[pl.ds(0, per), pl.ds(0, 3)])
        left("o", att_out.at[pl.ds(0, per), pl.ds(0, 3)])

    def start_tokens():
        loads[0].wait()
        pl.semaphore_wait(barrier, len(others))
        send("t", "t", tok.at[pl.ds(0, 128)], tok.at[pl.ds(rows, 128)], at_zl)

    def project_keys():
        loads[1].wait()
        loads[2].wait()
        project(wkv, 0, k_mine)
        kv_send("k", 0)

    def project_query():
        loads[3].wait()
        project(wq, 0, q_mine, scale)

    def project_values():
        loads[4].wait()
        project(wkv, half, v_mine)

    start_tokens()
    project_keys()
    kv_own("k", 0)
    project_query()
    q_send(0)
    project_values()
    kv_own("k", 2)
    kv_send("k", 1)
    kv_own("k", 1)
    kv_more("k")
    q_send(1)
    kv_forward("k", 0)
    kv_send("k", 2)
    kv_forward("k", 1)
    logits_mine(0)
    kv_own("v", 1)
    q_send(2)
    kv_last("k", 0)
    kv_own("v", 0)
    logits_theirs(0)
    add_mine(0)
    kv_send("v", 0)
    logits_mine(1)
    kv_last("k", 1)
    kv_forward("k", 2)
    add_theirs(0)
    logits_theirs(1)
    kv_send("v", 1)
    kv_more("v")
    logits_mine(2)
    add_mine(1)
    swap_weights()
    add_theirs(1)
    kv_last("k", 2)
    kv_forward("v", 0)
    logits_theirs(2)
    drain_keys()
    softmax(0)
    kv_send("v", 2)
    add_mine(2)
    add_theirs(2)
    softmax(1)
    kv_forward("v", 1)
    forward_probs(0)
    kv_last("v", 0)
    forward_probs(1)
    kv_forward("v", 3)
    kv_own("v", 3)
    kv_own("v", 4)
    kv_forward("v", 4)
    softmax(2)
    attend(0)
    kv_last("v", 1)
    forward_probs(2)
    attend(1)
    drain_most()
    kv_last("v", 3)
    attend(3)
    kv_last("v", 4)
    attend(4)
    project_out(0)
    project_out(1)
    project_out(3)
    project_out(4)

    drain_last()


def local(tokens, w_query, w_keyval, w_out):
    seq_dev, res_dev, width = tokens.shape
    heads = width // DH
    per = heads // NX
    scale = 1.0 / math.sqrt(DH * seq_dev * lax.axis_size("seq"))
    rows = seq_dev * res_dev
    block = (heads, res_dev, seq_dev * DH)
    mixed = pl.pallas_call(
        functools.partial(layer_kernel, scale),
        out_shape=jax.ShapeDtypeStruct((seq_dev // 2, 2, res_dev, width), F32),
        in_specs=[pl.BlockSpec(memory_space=pltpu.HBM)] * 4,
        out_specs=pl.BlockSpec(memory_space=pltpu.VMEM),
        scratch_shapes=[
            pltpu.VMEM((rows + 128, width), BF16),
            pltpu.VMEM((width, width), BF16),
            pltpu.VMEM((width, 2 * width), BF16),
            pltpu.VMEM((2, per, NX, DH, width), BF16),
            pltpu.VMEM(block, BF16),
            pltpu.VMEM(block, BF16),
            pltpu.VMEM(block, BF16),
            pltpu.VMEM((heads, res_dev, MORE), BF16),
            pltpu.VMEM((heads, res_dev, MORE), BF16),
            pltpu.VMEM((per, NX, res_dev, seq_dev * DH), BF16),
            pltpu.VMEM((per, 4, NX, res_dev, seq_dev * DH), BF16),
            pltpu.VMEM((per, 4, NX, res_dev, seq_dev * DH), BF16),
            pltpu.VMEM((NX, res_dev, 512), F32),
            pltpu.VMEM((per, 2, NY, res_dev, 512), BF16),
            pltpu.VMEM((per, 2, 3, res_dev, 512), BF16),
            pltpu.VMEM((per, 2, res_dev, 512), F32),
            pltpu.VMEM((per, 2, res_dev, 512), BF16),
            pltpu.VMEM((per, 2, res_dev, 512), BF16),
            pltpu.VMEM((per, NY, res_dev, 1024), BF16),
            pltpu.VMEM((per, NX, res_dev, seq_dev * DH), BF16),
            pltpu.VMEM(block, BF16),
            pltpu.VMEM((2, seq_dev // 2, res_dev, NX * DH), BF16),
            pltpu.SemaphoreType.DMA((8,)),
            pltpu.SemaphoreType.DMA((15,)),
            pltpu.SemaphoreType.DMA((54,)),
        ],
        cost_estimate=pl.CostEstimate(flops=6 * 10**9, bytes_accessed=10**7, transcendentals=2 * 10**5),
        compiler_params=pltpu.CompilerParams(
            collective_id=0, has_side_effects=True, vmem_limit_bytes=44 * 2**20
        ),
        name="tied_row_attention",
    )(*[pltpu.with_memory_space_constraint(a, pltpu.HBM) for a in (tokens.reshape(rows, width), w_query, w_keyval, w_out.reshape(NX, per, DH, width))])
    return mixed.reshape(seq_dev, res_dev, width)


def solution(mesh):
    return jax.shard_map(
        local,
        mesh=mesh,
        in_specs=(P("seq", "res", None), P(), P(), P()),
        out_specs=P("seq", "res", None),
        check_vma=False,
    )
```

```python
import functools
import math

import jax
import jax.numpy as jnp
from jax import lax
from jax.experimental import pallas as pl
from jax.experimental.pallas import tpu as pltpu
from jax.sharding import PartitionSpec as P

DH = 64
NX, NY = 4, 4
COLS = 256
MORE = 128
MESH = pl.DeviceIdType.MESH
BF16, F32 = jnp.bfloat16, jnp.float32


def layer_kernel(
    scale,
    tok_hbm, wq_hbm, wkv_hbm, wout_ref, out_ref,
    tok, wq, wkv, wout, q_mine, k_mine, v_mine, k_more, v_more, q_all, k_all, v_all,
    scores, part_out, part_in, own_rows, pair_out, pair_in, probs, att_out, att_all, lhs,
    load_sem, send_sem, recv_sem,
):
    seq, res = lax.axis_index("seq"), lax.axis_index("res")
    y, zh = lax.div(seq, 2), lax.rem(seq, 2)
    zl, x, c = lax.div(res, 8), lax.rem(lax.div(res, 2), NX), lax.rem(res, 2)
    rows, width = tok_hbm.shape
    heads = q_mine.shape[0]
    per = heads // NX

    def at_x(k):
        return (seq, zl * 8 + lax.rem(x + k, NX) * 2 + c)

    def at_y(k):
        return (lax.rem(y + k, NY) * 2 + zh, res)

    at_zl = (seq, (1 - zl) * 8 + x * 2 + c)
    at_core = (seq, zl * 8 + x * 2 + (1 - c))
    at_zh = (y * 2 + (1 - zh), res)

    senders, receivers, seen = {}, {}, set()

    def send(kind, group, src, dst, where, when=None):
        copy = pltpu.make_async_remote_copy(
            src_ref=src, dst_ref=dst,
            send_sem=send_sem.at[senders.setdefault(kind, len(senders))],
            recv_sem=recv_sem.at[receivers.setdefault(group, len(receivers))],
            device_id=where, device_id_type=MESH,
        )
        if when is None:
            copy.start()
        else:
            pl.when(when)(copy.start)

    def arrived(group, ref):
        if group not in seen:
            seen.add(group)
            pltpu.make_async_copy(ref, ref, recv_sem.at[receivers[group]]).wait()

    def left(kind, ref):
        pltpu.make_async_copy(ref, ref, send_sem.at[senders[kind]]).wait()

    half = wkv.shape[1] // 2
    loads = [
        pltpu.make_async_copy(tok_hbm.at[pl.ds(0, 128)], tok.at[pl.ds(0, 128)], load_sem.at[0]),
        pltpu.make_async_copy(tok_hbm.at[pl.ds(128, rows - 128)], tok.at[pl.ds(128, rows - 128)], load_sem.at[1]),
        pltpu.make_async_copy(wkv_hbm.at[:, pl.ds(0, half)], wkv.at[:, pl.ds(0, half)], load_sem.at[2]),
        pltpu.make_async_copy(wq_hbm, wq, load_sem.at[3]),
        pltpu.make_async_copy(wkv_hbm.at[:, pl.ds(half, half)], wkv.at[:, pl.ds(half, half)], load_sem.at[4]),
    ] + [pltpu.make_async_copy(wout_ref.at[:, hh], wout.at[0, hh], load_sem.at[5 + hh]) for hh in range(per)]
    for load in loads[:3]:
        load.start()

    barrier = pltpu.get_barrier_semaphore()
    others = [at_x(1), at_x(2), at_x(3), at_y(1), at_y(2), at_y(3), at_zl, at_core, at_zh]
    for other in others:
        pl.semaphore_signal(barrier, inc=1, device_id=other, device_id_type=MESH)
    for load in loads[3:]:
        load.start()

    low = lax.broadcasted_iota(jnp.int32, (64, 128), 1) < DH
    lows = jnp.where(low, 1.0, 0.0).astype(BF16)
    highs = jnp.where(low, 0.0, 1.0).astype(BF16)

    def project(w, first, dst, factor=None, row=0, pairs=rows // 128, after=None):
        def tile(n):
            at = first + n * COLS if after else pl.multiple_of(first + n * COLS, COLS)
            acc = jnp.dot(tok[row:row + pairs * 128], w[:, pl.ds(at, COLS)], preferred_element_type=F32)
            if factor is not None:
                acc = acc * factor
            for pair in range(COLS // 128):
                for m in range(pairs):
                    even = acc[m * 128:m * 128 + 64, pair * 128:pair * 128 + 128]
                    odd = pltpu.roll(acc[m * 128 + 64:m * 128 + 128, pair * 128:pair * 128 + 128], 64, 1)
                    head = n * (COLS // DH) + 2 * pair
                    dst[head, :, m * 128:m * 128 + 128] = jnp.where(low, even, odd).astype(BF16)
                    dst[head + 1, :, m * 128:m * 128 + 128] = jnp.where(low, odd, even).astype(BF16)

        if after is None:
            pl.loop(0, width // COLS)(tile)
        else:
            for n in range(width // COLS):
                tile(n)
                after(n)

    mine = zl * 2 + c
    theirs = (1 - zl) * 2 + c
    kv = {"k": (k_mine, k_all, k_more), "v": (v_mine, v_all, v_more)}

    def columns(stage):
        return {2: (2, 0, width), 3: (2, 0, 512), 4: (2, 512, 256)}.get(stage, (stage, 0, width))

    def kv_send(kind, hh):
        src, dst, _ = kv[kind]
        dst[hh, mine, x] = src[per * x + hh]
        for k in (1, 3, 2):
            to = lax.rem(x + k, NX)
            group = (kind + "x", hh, k if kind == "k" else 0)
            send(kind + "x", group, src.at[per * to + hh], dst.at[hh, mine, x], at_x(k))

    def kv_more(kind):
        arrived("t", tok.at[pl.ds(rows, 128)])
        _, dst, src = kv[kind]
        project(wkv, 0 if kind == "k" else half, src, row=rows, pairs=1)
        for hh in range(per):
            dst[hh, theirs, x, :, 0:MORE] = src[per * x + hh]
        for k in (2, 1, 3):
            to = lax.rem(x + k, NX)
            send(
                kind + "t", kind + "t", src.at[pl.ds(per * to, per)],
                dst.at[pl.ds(0, per), theirs, x, :, pl.ds(0, MORE)], at_x(k),
            )

    def across(stage):
        hh, lo, n = columns(stage)
        first = max(lo, MORE)
        return hh, pl.ds(first, lo + n - first)

    def kv_own(kind, stage):
        src, dst, _ = kv[kind]
        hh, at = across(stage)
        send(kind + "z", (kind + "z", stage), src.at[per * x + hh, :, at], dst.at[hh, mine, x, :, at], at_zl)

    def kv_forward(kind, stage):
        _, dst, _ = kv[kind]
        hh, at = across(stage)
        for k in (1, 3, 2):
            block = dst.at[hh, mine, lax.rem(x + NX - k, NX)]
            if kind == "k":
                arrived(("kx", hh, k), block)
            else:
                arrived(("vx", hh, 0), dst.at[hh, mine, pl.ds(0, 3)])
            block = block.at[:, at]
            send(kind + "z", (kind + "z", stage), block, block, at_zl)
        hh, lo, n = columns(stage)
        blocks = dst.at[hh, mine, :, :, pl.ds(lo, n)]
        send(kind + "c", (kind + "c", stage, 0), blocks, blocks, at_core)

    def kv_last(kind, stage):
        _, dst, _ = kv[kind]
        arrived(kind + "t", dst.at[pl.ds(0, per), theirs, pl.ds(0, 3), :, pl.ds(0, MORE)])
        hh, at = across(stage)
        arrived((kind + "z", stage), dst.at[hh, theirs, :, :, at])
        hh, lo, n = columns(stage)
        at = pl.ds(lo, n)
        blocks = dst.at[hh, theirs, :, :, at]
        if kind == "k":
            send("kc", ("kc", stage, 1), blocks, blocks, at_core)
            arrived(("kc", stage, 0), dst.at[hh, 2 * zl + 1 - c])
            arrived(("kc", stage, 1), dst.at[hh, 2 * (1 - zl) + 1 - c])
        else:
            send("vc", ("vc", stage, 0), blocks, blocks, at_core)
            arrived(("vc", stage, 0), dst.at[hh, pl.ds(0, 2), :, :, at])

    def q_send(hh):
        q_all[hh, x] = q_mine[per * x + hh]
        for k in (2, 1, 3):
            to = lax.rem(x + k, NX)
            send("q", ("q", hh), q_mine.at[per * to + hh], q_all.at[hh, x], at_x(k))

    def logits(hh, half):
        arrived(("q", hh), q_all.at[hh, pl.ds(0, 3)])

        @pl.loop(0, 2)
        def _(t):
            s = lax.dot_general(
                q_all[hh].reshape(256, width), k_all[hh, half * 2 + t].reshape(256, width),
                (((1,), (1,)), ((), ())), preferred_element_type=F32,
            ).reshape(NX, 64, 256)
            at = pl.ds(pl.multiple_of(t * 256, 256), 256)
            scores[:, :, at] = s
            part_out[hh, half, :, :, at] = s.astype(BF16)

        own_rows[hh, half] = scores[y]

    def send_rows(kind, hh, half):
        for k in (2, 1, 3):
            send(
                kind, (kind, hh), part_out.at[hh, half, lax.rem(y + k, NY)], part_in.at[hh, half, k - 1], at_y(k)
            )

    def logits_mine(hh):
        arrived(("kc", hh, 0), k_all.at[hh, 2 * zl + 1 - c])
        logits(hh, zl)
        send_rows("s", hh, zl)

    def logits_theirs(hh):
        logits(hh, 1 - zl)
        send_rows("r", hh, 1 - zl)

    def add_rows(hh, kind, half):
        arrived((kind, hh), part_in.at[hh, half])
        total = own_rows[hh, half]
        for k in range(3):
            total = total + part_in[hh, half, k].astype(F32)
        own_rows[hh, half] = total
        pair_out[hh, half] = total.astype(BF16)
        send("p", ("p", hh), pair_out.at[hh, half], pair_in.at[hh, half], at_zh)

    def add_mine(hh):
        add_rows(hh, "s", zl)

    def add_theirs(hh):
        add_rows(hh, "r", 1 - zl)

    def softmax(hh):
        arrived(("p", hh), pair_in.at[hh])
        totals = [own_rows[hh, half] + pair_in[hh, half].astype(F32) for half in range(2)]
        largest = jnp.max(jnp.maximum(totals[0], totals[1]), axis=-1, keepdims=True)
        weights = [jnp.exp(total - largest) for total in totals]
        scaling = 1.0 / jnp.sum(weights[0] + weights[1], axis=-1, keepdims=True)
        for half in range(2):
            probs[hh, y, :, half * 512:half * 512 + 512] = (weights[half] * scaling).astype(BF16)
        for kind, first in (("a", 0), ("b", 32)):
            for k in (1, 3):
                block = probs.at[hh, y, pl.ds(first if k == 1 else 32 - first, 32)]
                send("a", (kind, hh), block, block, at_y(k))

    def forward_probs(hh):
        for k, first in ((1, 0), (3, 32)):
            arrived(("a", hh), probs.at[hh, 0])
            block = probs.at[hh, lax.rem(y + NY - k, NY), pl.ds(first, 32)]
            send("a", ("b", hh), block, block, at_y(k))

    def attend(stage):
        hh, lo, n = columns(stage)
        arrived(("a", hh), probs.at[hh, 0])
        arrived(("b", hh), probs.at[hh, pl.ds(0, 2)])

        @pl.loop(lo // COLS, (lo + n) // COLS)
        def _(tile):
            at = pl.ds(pl.multiple_of(tile * COLS, COLS), COLS)
            o = jnp.dot(
                probs[hh].reshape(256, 1024), v_all[hh, :, :, :, at].reshape(1024, COLS),
                preferred_element_type=F32,
            )
            att_out[hh, :, :, at] = o.astype(BF16).reshape(NX, 64, COLS)

        at = pl.ds(lo, n)
        att_all[per * x + hh, :, at] = att_out[hh, x, :, at]
        for k in (2, 1, 3):
            to = lax.rem(x + k, NX)
            send("o", ("o", stage), att_out.at[hh, to, :, at], att_all.at[per * x + hh, :, at], at_x(k))

    def swap_weights():
        for load in loads[5:]:
            load.wait()
        for hh in range(per):
            for xp in range(NX):
                wout[1, hh, xp] = wout[0, hh, xp ^ 1]

    def project_out(stage):
        hh, lo, n = columns(stage)
        arrived(("o", stage), att_all.at[pl.ds(0, 3), :, pl.ds(lo, n)])
        m0, m1 = lo // 128, (lo + n) // 128
        for m in range(m0, m1):
            for pair in range(NX // 2):
                a = att_all[2 * pair * per + hh, :, m * 128:m * 128 + 128]
                b = att_all[(2 * pair + 1) * per + hh, :, m * 128:m * 128 + 128]
                lhs[0, m, :, pair * 128:pair * 128 + 128] = a * lows + b * highs
                lhs[1, m, :, pair * 128:pair * 128 + 128] = b * lows + a * highs

        @pl.loop(0, width // COLS)
        def _(tile):
            at = pl.ds(pl.multiple_of(tile * COLS, COLS), COLS)
            for q in range(2):
                s = (hh + q) % 2
                o = jnp.dot(
                    lhs[q, m0:m1].reshape((m1 - m0) * 64, NX * DH), wout[q, hh, :, :, at].reshape(NX * DH, COLS),
                    preferred_element_type=F32,
                ).reshape(m1 - m0, 64, COLS)
                out_ref[m0:m1, s, :, at] = o if hh == 0 else out_ref[m0:m1, s, :, at] + o

    def drain_keys():
        across_z = pl.ds(MORE, width - MORE)
        left("t", tok.at[pl.ds(0, 128)])
        left("kx", k_mine.at[pl.ds(0, 3 * per)])
        left("kt", k_more.at[pl.ds(0, 3 * per)])
        left("kz", k_mine.at[pl.ds(0, 4 * per), :, across_z])
        left("kc", k_all.at[pl.ds(0, per), pl.ds(0, 2)])
        left("q", q_mine.at[pl.ds(0, 3 * per)])
        for kind in ("r", "s"):
            left(kind, part_out.at[pl.ds(0, per), 0, pl.ds(0, 3)])

    def drain_most():
        left("vx", v_mine.at[pl.ds(0, 3 * per)])
        left("vt", v_more.at[pl.ds(0, 3 * per)])
        left("p", pair_out)

    def drain_last():
        left("vz", v_mine.at[pl.ds(0, 4 * per), :, pl.ds(MORE, width - MORE)])
        left("vc", v_all.at[pl.ds(0, per), pl.ds(0, 2)])
        left("a", probs.at[pl.ds(0, per), pl.ds(0, 3)])
        left("o", att_out.at[pl.ds(0, per), pl.ds(0, 3)])

    def start_tokens():
        loads[0].wait()
        pl.semaphore_wait(barrier, len(others))
        send("t", "t", tok.at[pl.ds(0, 128)], tok.at[pl.ds(rows, 128)], at_zl)

    def project_keys():
        loads[1].wait()
        loads[2].wait()
        project(wkv, 0, k_mine)
        kv_send("k", 0)

    def project_query():
        loads[3].wait()
        project(wq, 0, q_mine, scale)

    def project_values():
        loads[4].wait()
        project(wkv, half, v_mine)

    start_tokens()
    project_keys()
    kv_own("k", 0)
    project_query()
    q_send(0)
    project_values()
    kv_own("k", 2)
    kv_send("k", 1)
    kv_own("k", 1)
    kv_more("k")
    q_send(1)
    kv_forward("k", 0)
    kv_send("k", 2)
    kv_forward("k", 1)
    logits_mine(0)
    kv_own("v", 1)
    q_send(2)
    kv_last("k", 0)
    kv_own("v", 0)
    logits_theirs(0)
    add_mine(0)
    kv_send("v", 0)
    logits_mine(1)
    kv_last("k", 1)
    kv_forward("k", 2)
    add_theirs(0)
    logits_theirs(1)
    kv_send("v", 1)
    kv_more("v")
    logits_mine(2)
    add_mine(1)
    swap_weights()
    add_theirs(1)
    kv_last("k", 2)
    kv_forward("v", 0)
    logits_theirs(2)
    drain_keys()
    softmax(0)
    kv_send("v", 2)
    add_mine(2)
    add_theirs(2)
    softmax(1)
    kv_forward("v", 1)
    forward_probs(0)
    kv_last("v", 0)
    forward_probs(1)
    kv_forward("v", 3)
    kv_own("v", 3)
    kv_own("v", 4)
    kv_forward("v", 4)
    softmax(2)
    attend(0)
    kv_last("v", 1)
    forward_probs(2)
    attend(1)
    drain_most()
    kv_last("v", 3)
    attend(3)
    kv_last("v", 4)
    attend(4)
    project_out(0)
    project_out(1)
    project_out(3)
    project_out(4)

    drain_last()


def local(tokens, w_query, w_keyval, w_out):
    seq_dev, res_dev, width = tokens.shape
    heads = width // DH
    per = heads // NX
    scale = 1.0 / math.sqrt(DH * seq_dev * lax.axis_size("seq"))
    rows = seq_dev * res_dev
    block = (heads, res_dev, seq_dev * DH)
    mixed = pl.pallas_call(
        functools.partial(layer_kernel, scale),
        out_shape=jax.ShapeDtypeStruct((seq_dev // 2, 2, res_dev, width), F32),
        in_specs=[pl.BlockSpec(memory_space=pltpu.HBM)] * 4,
        out_specs=pl.BlockSpec(memory_space=pltpu.VMEM),
        scratch_shapes=[
            pltpu.VMEM((rows + 128, width), BF16),
            pltpu.VMEM((width, width), BF16),
            pltpu.VMEM((width, 2 * width), BF16),
            pltpu.VMEM((2, per, NX, DH, width), BF16),
            pltpu.VMEM(block, BF16),
            pltpu.VMEM(block, BF16),
            pltpu.VMEM(block, BF16),
            pltpu.VMEM((heads, res_dev, MORE), BF16),
            pltpu.VMEM((heads, res_dev, MORE), BF16),
            pltpu.VMEM((per, NX, res_dev, seq_dev * DH), BF16),
            pltpu.VMEM((per, 4, NX, res_dev, seq_dev * DH), BF16),
            pltpu.VMEM((per, 4, NX, res_dev, seq_dev * DH), BF16),
            pltpu.VMEM((NX, res_dev, 512), F32),
            pltpu.VMEM((per, 2, NY, res_dev, 512), BF16),
            pltpu.VMEM((per, 2, 3, res_dev, 512), BF16),
            pltpu.VMEM((per, 2, res_dev, 512), F32),
            pltpu.VMEM((per, 2, res_dev, 512), BF16),
            pltpu.VMEM((per, 2, res_dev, 512), BF16),
            pltpu.VMEM((per, NY, res_dev, 1024), BF16),
            pltpu.VMEM((per, NX, res_dev, seq_dev * DH), BF16),
            pltpu.VMEM(block, BF16),
            pltpu.VMEM((2, seq_dev // 2, res_dev, NX * DH), BF16),
            pltpu.SemaphoreType.DMA((8,)),
            pltpu.SemaphoreType.DMA((15,)),
            pltpu.SemaphoreType.DMA((54,)),
        ],
        cost_estimate=pl.CostEstimate(flops=6 * 10**9, bytes_accessed=10**7, transcendentals=2 * 10**5),
        compiler_params=pltpu.CompilerParams(
            collective_id=0, has_side_effects=True, vmem_limit_bytes=44 * 2**20
        ),
        name="tied_row_attention",
    )(*[pltpu.with_memory_space_constraint(a, pltpu.HBM) for a in (tokens.reshape(rows, width), w_query, w_keyval, w_out.reshape(NX, per, DH, width))])
    return mixed.reshape(seq_dev, res_dev, width)


def solution(mesh):
    return jax.shard_map(
        local,
        mesh=mesh,
        in_specs=(P("seq", "res", None), P(), P(), P()),
        out_specs=P("seq", "res", None),
        check_vma=False,
    )
```
